32 devices in a mesh: dp: 8 (over z, y), tensor: 4 (over x, core).
Axes of the slice: x: 2, y: 2, z: 4, core: 2. Of those that a mesh axis runs over, the one named last changes fastest.
Arguments:
- stream: bfloat16 [32768, 767], P(('dp', 'tensor')), may hold values from -6 to 6
- cotangent: bfloat16 [32768, 767], P(('dp', 'tensor')), may hold values from -6 to 6
- bucket: int32 [8], P('dp'), may hold values from 0 to 2, as said below
- row_counts: int32 [8], P('dp'), may hold values from 1 to 4, as said below
- lengths: int32 [8, 4], P('dp'), may hold values from 0 to 4096, as said below
- w_qkv: bfloat16 [768, 3, 768], P(None, None, 'tensor'), may hold values from -0.3125 to 0.3125
- w_out: bfloat16 [768, 768], P('tensor'), may hold values from -0.75 to 0.75
- w_up: bfloat16 [768, 3072], P(None, 'tensor'), may hold values from -0.21875 to 0.21875
- w_down: bfloat16 [3072, 768], P('tensor'), may hold values from -0.109375 to 0.109375
- gain_one: float32 [768], replicated, may hold values from 0.5 to 1.5
- gain_two: float32 [768], replicated, may hold values from 0.5 to 1.5
Outputs:
- result: bfloat16 [32768, 767], P(('dp', 'tensor'))
- grad_stream: float32 [32768, 767], P(('dp', 'tensor'))
- grad_w_qkv: float32 [768, 3, 768], P(None, None, 'tensor')
- grad_w_out: float32 [768, 768], P('tensor')
- grad_w_up: float32 [768, 3072], P(None, 'tensor')
- grad_w_down: float32 [3072, 768], P('tensor')
- grad_gain_one: float32 [768], replicated
- grad_gain_two: float32 [768], replicated
- root_means: float32 [3], replicated
The draws below stay inside these ranges and needn't reach their ends.
Inputs may be any that keep to these rules, and one draw needn't show every extreme that they name: Rows of group g have 1024 * 2**bucket[g] slots. row_counts[g] is at most 4096 // (1024 * 2**bucket[g]) and at least half of that. lengths[g, r] lies between half the row's span and the span for r below row_counts[g], and is 0 from there on; the first row of every group is full.
All inputs are finite; a program needn't handle non-finite values.
Results may differ from the reference program's by a relative error of at most 0.013.
The reference program's roundings to bfloat16 on the way count: a program that leaves them out, or rounds other values in their place, can miss the bound.
Values may be sent and summed in bfloat16 or wider, within the bound.
No kernel may reach another device: no remote copies, remote signals or barrier semaphores. Data moves between devices by JAX's collectives and lax.ppermute only.
A program may use at most 256 MiB of HBM per device.

```python
import jax
import jax.numpy as jnp
from jax import lax

D = 768
HEADS = 12
HD = 64
FF = 3072
BASE = 1024
TOK_GRP = 4096
DC = 767
SLOTS = 4
TOKENS = 32768
N_DP = 8


def span_factor(bucket_all):
    return jnp.where(bucket_all == 0, 1, jnp.where(bucket_all == 1, 2, 4)).astype(jnp.int32)


def group_plan(key):
    shuffled = jax.random.permutation(jax.random.fold_in(key, 41), N_DP)
    bucket_all = jax.random.randint(jax.random.fold_in(key, 42), (N_DP,), 0, 3, dtype=jnp.int32)
    bucket_all = bucket_all.at[shuffled[0]].set(2).at[shuffled[1]].set(0)
    row_limit = TOK_GRP // (BASE * span_factor(bucket_all))
    removed = jax.random.randint(jax.random.fold_in(key, 43), (N_DP,), 0, row_limit // 2 + 1, dtype=jnp.int32)
    removed = jnp.where(jnp.arange(N_DP, dtype=jnp.int32) == shuffled[1], 0, removed)
    return (bucket_all.astype(jnp.int32), (row_limit - removed).astype(jnp.int32))


def draw_bucket(key, part):
    bucket_all, count_all = group_plan(key)
    return bucket_all


def draw_row_counts(key, part):
    bucket_all, count_all = group_plan(key)
    return count_all


def draw_lengths(key, part):
    bucket_all, count_all = group_plan(key)
    key = jax.random.fold_in(key, 7)
    row_span = BASE * span_factor(bucket_all)
    shortfall = jax.random.randint(key, (N_DP, SLOTS), 0, (row_span // 2)[:, None], dtype=jnp.int32)
    slot_index = jnp.arange(SLOTS, dtype=jnp.int32)[None, :]
    length_all = jnp.where(slot_index == 0, row_span[:, None], row_span[:, None] - shortfall)
    return jnp.where(slot_index < count_all[:, None], length_all, 0).astype(jnp.int32)


def level_of(rng, shape, cuts, least, top_value):
    level, own = 1.0, jax.random.fold_in(rng, 6)
    for dim, parts in cuts:
        draws = jnp.exp(jax.random.uniform(jax.random.fold_in(own, dim), (parts,), jnp.float32, least / len(cuts), top_value / len(cuts)))
        level = level * jnp.repeat(draws, shape[dim] // parts).reshape([-1 if axis == dim else 1 for axis in range(len(shape))])
    return level


def normal_values(stream_key, extent, scale, limit, shards=(), kind=jnp.bfloat16):
    entries = jax.random.normal(stream_key, extent, jnp.float32) * scale
    if len(shards) > 0:
        entries = level_of(stream_key, extent, shards, -0.22, 0.18) * entries
    return jnp.clip(entries, min=-limit, max=limit).astype(kind)


def setup_inputs(seed: int = 0) -> dict:
    arg_keys = jax.random.split(jax.random.key(seed), 12)
    stream = normal_values(arg_keys[0], (TOKENS, DC), 1.0, 6.0, ((0, 32),))
    cotangent = normal_values(arg_keys[1], (TOKENS, DC), 1.0, 6.0, ((0, 32),))
    bucket = draw_bucket(jax.random.fold_in(arg_keys[11], 71), 0)
    row_counts = draw_row_counts(jax.random.fold_in(arg_keys[11], 71), 0)
    lengths = draw_lengths(jax.random.fold_in(arg_keys[11], 71), 0)
    w_qkv = normal_values(arg_keys[5], (D, 3, D), (D // 2) ** -0.5, 0.3125, ((2, 4),))
    w_out = normal_values(arg_keys[6], (D, D), HD ** -0.5, 0.75, ((0, 4),))
    w_up = normal_values(arg_keys[7], (D, FF), D ** -0.5, 0.21875, ((1, 4),))
    w_down = normal_values(arg_keys[8], (FF, D), FF ** -0.5, 0.109375, ((0, 4),))
    gain_one = jnp.clip(1.0 + 0.1 * jax.random.normal(arg_keys[9], (D,), jnp.float32), 0.5, 1.5)
    gain_two = jnp.clip(1.0 + 0.1 * jax.random.normal(arg_keys[10], (D,), jnp.float32), 0.5, 1.5)
    return {"stream": stream, "cotangent": cotangent, "bucket": bucket, "row_counts": row_counts, "lengths": lengths, "w_qkv": w_qkv, "w_out": w_out, "w_up": w_up, "w_down": w_down, "gain_one": gain_one, "gain_two": gain_two}


EPSILON = 1e-05

@jax.custom_vjp
def low(v):
    return lax.optimization_barrier(v.astype(jnp.bfloat16)).astype(jnp.float32)

@jax.custom_vjp
def low_back(v):
    return v

def low_keep(v):
    return (low(v), None)

def low_pass(kept, grad):
    return (grad,)

def back_keep(v):
    return (v, None)

def back_low(kept, grad):
    return (low(grad),)
low.defvjp(low_keep, low_pass)
low_back.defvjp(back_keep, back_low)

def highest(form, left, right):
    return jnp.einsum(form, left, right, precision=lax.Precision.HIGHEST)

def decompress(narrow):
    return jnp.concatenate([narrow, -lax.optimization_barrier(jnp.sum(narrow, axis=1, keepdims=True))], axis=1)

def compress(branch):
    centred = branch - lax.optimization_barrier(jnp.mean(branch, axis=1, keepdims=True))
    return centred[:, :-1]

def crms(narrow, gain):
    full = decompress(narrow)
    factor = lax.rsqrt(lax.optimization_barrier(jnp.mean(full * full, axis=1, keepdims=True)) + EPSILON)
    return full * factor * gain

def layout(bucket_one, count_one, length_one, slot_total):
    row_span = BASE * jnp.where(bucket_one == 0, 1, jnp.where(bucket_one == 1, 2, 4)).astype(jnp.int32)
    place = jnp.arange(slot_total, dtype=jnp.int32)
    row_of = place // row_span
    pos_in = place % row_span
    slot_index = jnp.arange(length_one.shape[0], dtype=jnp.int32)
    row_len = lax.optimization_barrier(jnp.sum(jnp.where(row_of[:, None] == slot_index[None, :], length_one[None, :], 0), axis=1))
    usable = (row_of < count_one) & (pos_in < row_len)
    return (row_of, pos_in, usable)

def forward(narrow, w_qkv, w_out, w_up, w_down, gain_one, gain_two, row_of, pos_in, usable):
    slot_total = narrow.shape[0]
    normed_one = low(crms(narrow, gain_one))
    packed = highest('td,dc->tc', normed_one, w_qkv.reshape(D, 3 * D))
    packed = low_back(low(packed)).reshape(slot_total, 3, HEADS, HD)
    query_all, key_all, value_all = (packed[:, 0], packed[:, 1], packed[:, 2])
    index_all = jnp.arange(slot_total, dtype=jnp.int32)
    block_rows = min(512, slot_total)
    block_count = slot_total // block_rows

    def blocked(array):
        return array.reshape((block_count, block_rows) + array.shape[1:])

    def attend(element):
        query_blk, row_q, pos_q, index_q = element
        scores = highest('bhd,khd->hbk', query_blk, key_all) * HD ** (-0.5)
        allowed_mask = (row_of[None, :] == row_q[:, None]) & (pos_in[None, :] <= pos_q[:, None]) & (usable[None, :] | (index_all[None, :] == index_q[:, None]))
        scores = low_back(jnp.where(allowed_mask[None], scores, -1e+30))
        probas = jax.nn.softmax(scores, axis=2)
        return highest('hbk,khd->bhd', low(probas), value_all)
    attn_blocks = lax.map(jax.checkpoint(attend), (blocked(query_all), blocked(row_of), blocked(pos_in), blocked(index_all)))
    attn_all = low_back(low(attn_blocks.reshape(slot_total, D)))
    branch_attn = low_back(highest('tc,cd->td', attn_all, w_out))
    middle = narrow + compress(branch_attn)
    normed_two = low(crms(middle, gain_two))
    pre_act = low_back(highest('td,df->tf', normed_two, w_up))
    hidden = low(jax.nn.gelu(pre_act))
    branch_mlp = low_back(highest('tf,fd->td', hidden, w_down))
    return (middle + compress(branch_mlp), (branch_attn, branch_mlp))

def reference(stream, cotangent, bucket, row_counts, lengths, w_qkv, w_out, w_up, w_down, gain_one, gain_two):
    params = (w_qkv.astype(jnp.float32), w_out.astype(jnp.float32), w_up.astype(jnp.float32), w_down.astype(jnp.float32), gain_one.astype(jnp.float32), gain_two.astype(jnp.float32))

    def group_step(carry, element):
        piece_in, piece_cot, bucket_one, count_one, length_one = element
        row_of, pos_in, usable = layout(bucket_one, count_one, length_one, TOK_GRP)

        def apply(narrow, *weights):
            return forward(narrow, *weights, row_of, pos_in, usable)
        out_f, pull, branches = jax.vjp(apply, piece_in.astype(jnp.float32), *params, has_aux=True)
        branch_attn, branch_mlp = branches
        weight_mask = usable.astype(jnp.float32)[:, None]
        grads = pull(piece_cot.astype(jnp.float32) * weight_mask)
        full_out = decompress(out_f)
        square_sums = jnp.stack([jnp.sum(full_out * full_out * weight_mask), jnp.sum(branch_attn * branch_attn * weight_mask), jnp.sum(branch_mlp * branch_mlp * weight_mask), jnp.sum(weight_mask)])
        updated = tuple((old + new for old, new in zip(carry, tuple(grads[1:]) + (square_sums,))))
        return (updated, (out_f.astype(jnp.bfloat16), grads[0]))
    initial = tuple((jnp.zeros(p.shape, jnp.float32) for p in params)) + (jnp.zeros((4,), jnp.float32),)
    inputs = (stream.reshape(N_DP, TOK_GRP, DC), cotangent.reshape(N_DP, TOK_GRP, DC), bucket, row_counts, lengths)
    totals, outputs = lax.scan(group_step, initial, inputs)
    result, grad_stream = outputs
    sums_all = totals[6]
    root_means = jnp.sqrt(sums_all[:3] / (D * sums_all[3]))
    return (result.reshape(TOKENS, DC), grad_stream.reshape(TOKENS, DC), totals[0], totals[1], totals[2], totals[3], totals[4], totals[5], root_means)
```

```python
import functools
import jax, jax.numpy as jnp, numpy as np
from jax import lax
from jax.experimental import pallas as pl
from jax.experimental.pallas import tpu as pltpu
from jax.sharding import PartitionSpec as P
HD=64; BASE=1024
LANES=128
SHIFT_LIMIT=70.0
F32=jnp.float32; BF=jnp.bfloat16
NT=(((1,),(1,)),((),()))
NN=(((1,),(0,)),((),()))
def dot(a,b,dims): return lax.dot_general(a,b,dims,preferred_element_type=F32)

def tables(nh, wide):
    cols=nh*HD; lane=np.arange(wide)
    head=np.where(lane<cols,lane//HD,np.where(lane<cols+4*nh,(lane-cols)//4,-1))
    spare=(lane>=cols)&(lane<cols+4*nh)
    masks=np.zeros((8,wide),np.float32)
    for h in range(nh): masks[h]=(head==h)
    masks[nh]=spare
    for h in range(nh): masks[nh+1+h]=spare&(head==h)
    fold=np.zeros((wide,LANES),np.float32)
    hi=wide-LANES
    same=(head[:,None]==head[None,hi:])&(head[:,None]>=0)
    fold[:]=same&(lane<cols)[:,None]&spare[None,hi:]
    spread=np.zeros((LANES,wide),np.float32)
    spread[:]=(same&(lane<cols)[:,None]&spare[None,hi:]).T
    return jnp.asarray(masks,BF),jnp.asarray(fold,BF),jnp.asarray(spread,BF)

def row_info(sc_ref, start):
    span=sc_ref[1]
    row=start//span
    length=sc_ref[3]
    for r in range(1,4):
        length=jnp.where(row==r, sc_ref[3+r], length)
    length=jnp.where(row<sc_ref[2], length, 0)
    return row*span, row*span+length, row*span+span

def place(sc_ref, start, shard):
    return pl.multiple_of((jnp.bitwise_xor(start//shard, sc_ref[0]))*shard + start%shard, 256)

def parts(x, cols, hi):
    lane=lax.broadcasted_iota(jnp.int32,x.shape,1)+hi-cols
    which=jnp.where(lane<0,3,lane%4)
    a=x.astype(BF).astype(F32); r=x-a; b=r.astype(BF).astype(F32); c=r-b
    return jnp.where(which==0,a,jnp.where(which==1,b,jnp.where(which==2,c,0.0))).astype(BF)

def fwd_kernel(nh, bq, shard, sc_ref, p_ref, mask_ref, fold_ref, spread_ref, o_ref, qx_ref, q_s, k_s, v_s, kn_s, sh_s, a_s):
    T=p_ref.shape[0]; W=p_ref.shape[1]//3; hi=W-LANES; cols=nh*HD
    i=pl.program_id(0)
    @pl.when(i==0)
    def _():
        kn=jnp.zeros((8,LANES),F32)
        for c in range(0,T,512):
            k=p_ref[c:c+512,W:2*W]; v=p_ref[c:c+512,2*W:]
            k_s[c:c+512,:]=k+mask_ref[nh:nh+1,:]
            kn=jnp.maximum(kn,jnp.max(dot(k*k,fold_ref[...],NN).reshape(64,8,LANES),axis=0))
            for h in range(nh):
                v_s[h,c:c+512,:]=v*mask_ref[h:h+1,:]+mask_ref[nh+1+h:nh+2+h,:]
        kn_s[...]=jnp.broadcast_to(jnp.max(kn,axis=0,keepdims=True),(8,LANES))
    start=i*bq
    row_start,valid_end,_=row_info(sc_ref,start)
    at=place(sc_ref,start,shard)
    q=p_ref[pl.ds(at,bq),:W]; own=p_ref[pl.ds(at,bq),W:2*W]
    before=(start-row_start)//bq
    full=jnp.minimum(before,(valid_end-row_start)//bq)
    some=jnp.minimum(before,(valid_end-row_start+bq-1)//bq)
    rows=lax.broadcasted_iota(jnp.int32,(bq,bq),0); tcol=lax.broadcasted_iota(jnp.int32,(bq,bq),1)
    diag=(tcol==rows)|((tcol<rows)&(tcol<valid_end-start))
    def set_q(shift_lanes):
        x=jnp.concatenate([q[:,:hi],q[:,hi:]+shift_lanes],axis=1)
        for h in range(nh): q_s[h]=x*mask_ref[h:h+1,:]
    self_score=dot(q*own,fold_ref[...],NN)
    shift=self_score.astype(BF).astype(F32)
    sh_s[...]=shift
    set_q(parts(-shift,cols,hi))
    size=jnp.sqrt(dot(q*q,fold_ref[...],NN)*kn_s[:1,:])*1.02
    bounded=jnp.max(size-shift)<=SHIFT_LIMIT
    @pl.when(jnp.logical_not(bounded))
    def _():
        lane=lax.broadcasted_iota(jnp.int32,(bq,LANES),1)+hi-cols
        new=jnp.zeros((bq,LANES),F32)
        for h in range(nh):
            qh=q*mask_ref[h:h+1,:]
            m0=jnp.max(jnp.where(diag,dot(qh,k_s[pl.ds(at,bq),:],NT),-1e30),axis=1,keepdims=True)
            def look(j,m):
                b=row_start+j*bq
                s=dot(qh,k_s[pl.ds(place(sc_ref,b,shard),bq),:],NT)
                s=jnp.where(tcol<valid_end-b,s,-1e30)
                return jnp.maximum(m,jnp.max(s,axis=1,keepdims=True))
            m=lax.fori_loop(0,some,look,m0)
            new=jnp.where((lane>=4*h)&(lane<4*h+4),m,new)
        sh_s[...]=new
        set_q(parts(-new,cols,hi))
    def step(b,masking,first):
        bt=place(sc_ref,b,shard)
        k=k_s[pl.ds(bt,bq),:]
        ps=[]
        for h in range(nh):
            s=dot(q_s[h],k,NT)
            if masking is not None: s=jnp.where(masking,s,-1e30)
            ps.append(jnp.exp(s).astype(BF))
        new=dot(jnp.concatenate(ps,axis=1),v_s[:,pl.ds(bt,bq),:].reshape(nh*bq,W),NN)
        if first: a_s[...]=new
        else: a_s[...]+=new
    step(start,diag,True)
    def whole(j,c):
        step(row_start+j*bq,None,False); return c
    def partly(j,c):
        b=row_start+j*bq
        step(b,tcol<valid_end-b,False); return c
    lax.fori_loop(0,full,whole,0)
    lax.fori_loop(full,some,partly,0)
    total=a_s[:,hi:]
    lane=lax.broadcasted_iota(jnp.int32,(bq,LANES),1)+hi-cols
    spare=(lane>=0)&(lane<4*nh)
    total=jnp.where(spare,total,1.0)
    o_ref[...]=(a_s[:,:cols]*dot(parts(1.0/total,cols,hi),spread_ref[...],NN)[:,:cols]).astype(BF)
    lse=jnp.where(spare,sh_s[...]+jnp.log(total),0.0)
    qx_ref[...]=jnp.concatenate([q[:,:hi],q[:,hi:]+parts(-lse,cols,hi)],axis=1)

def const(a): return pl.BlockSpec(a.shape,lambda i,sc:(0,)*a.ndim)

def attn_fwd(scal, packed, shard, nh=3, bq=512):
    T=packed.shape[0]; W=packed.shape[1]//3
    tabs=tables(nh,W)
    def where(i,sc):
        per=shard//bq
        return (jnp.bitwise_xor(i//per,sc[0])*per+i%per,0)
    return pl.pallas_call(
        functools.partial(fwd_kernel,nh,bq,shard),
        grid_spec=pltpu.PrefetchScalarGridSpec(num_scalar_prefetch=1,grid=(T//bq,),
            in_specs=[const(packed)]+[const(a) for a in tabs],
            out_specs=[pl.BlockSpec((bq,nh*HD),where),pl.BlockSpec((bq,W),where)],
            scratch_shapes=[pltpu.VMEM((nh,bq,W),BF),pltpu.VMEM((T,W),BF),pltpu.VMEM((nh,T,W),BF),
                pltpu.VMEM((8,LANES),F32),pltpu.VMEM((bq,LANES),F32),pltpu.VMEM((bq,W),F32)]),
        out_shape=[jax.ShapeDtypeStruct((T,nh*HD),BF),jax.ShapeDtypeStruct((T,W),BF)],
        compiler_params=pltpu.CompilerParams(vmem_limit_bytes=56*2**20),
        name="attention_forward",
    )(scal,packed,*tabs)

def bwd_kernel(nh,bk,shard,sc_ref,qx_ref,p_ref,o_ref,g_ref,mask_ref,fold_ref,out_ref,q_s,d_s,dq_s,dk_s,dv_s):
    T=p_ref.shape[0]; W=p_ref.shape[1]//3; hi=W-LANES; cols=nh*HD
    j=pl.program_id(0)
    @pl.when(j==0)
    def _():
        for c in range(0,T,512):
            qx=qx_ref[c:c+512,:]
            g=g_ref[c:c+512,:]
            og=o_ref[c:c+512,:].astype(F32)*g.astype(F32)
            og1=og.astype(BF); og2=(og-og1.astype(F32)).astype(BF)
            delta=dot(og1,fold_ref[:cols,:],NN)+dot(og2,fold_ref[:cols,:],NN)
            gx=jnp.concatenate([g,jnp.zeros((512,W-cols),BF)],axis=1)
            gx=jnp.concatenate([gx[:,:hi],gx[:,hi:]+parts(-delta,cols,hi)],axis=1)
            for h in range(nh):
                q_s[h,c:c+512,:]=qx*mask_ref[h:h+1,:]
                d_s[h,c:c+512,:]=gx*mask_ref[h:h+1,:]
            dq_s[:,c:c+512]=jnp.zeros((cols,512),F32)
    start=j*bk
    row_start,valid_end,row_end=row_info(sc_ref,start)
    at=place(sc_ref,start,shard)
    k0=p_ref[pl.ds(at,bk),W:2*W]
    k=k0+mask_ref[nh:nh+1,:]; v=p_ref[pl.ds(at,bk),2*W:]+mask_ref[nh:nh+1,:]
    kt=jnp.transpose(k0)
    def step(i,kind):
        b=start+i*bk
        bt=place(sc_ref,b,shard)
        if kind!=0:
            krow=lax.broadcasted_iota(jnp.int32,(bk,bk),0); qcol=lax.broadcasted_iota(jnp.int32,(bk,bk),1)
            ok=krow<valid_end-start
            if kind==2: ok=(krow==qcol)|((krow<qcol)&ok)
        ps=[];dss=[]
        for h in range(nh):
            s=dot(k,q_s[h,pl.ds(bt,bk),:],NT)
            if kind!=0: s=jnp.where(ok,s,-1e30)
            p=jnp.exp(s)
            ds=(p*dot(v,d_s[h,pl.ds(bt,bk),:],NT)).astype(BF)
            ps.append(p.astype(BF)); dss.append(ds)
            dq_s[h*HD:(h+1)*HD,pl.ds(bt,bk)]+=dot(kt[h*HD:(h+1)*HD],ds,NN)
        dv=dot(jnp.concatenate(ps,axis=1),d_s[:,pl.ds(bt,bk),:].reshape(nh*bk,W),NN)
        dk=dot(jnp.concatenate(dss,axis=1),q_s[:,pl.ds(bt,bk),:].reshape(nh*bk,W),NN)
        if kind==2: dv_s[...]=dv; dk_s[...]=dk
        else: dv_s[...]+=dv; dk_s[...]+=dk
    after=(row_end-start)//bk
    n_off=jnp.where(valid_end>start,after,1)
    step(0,2)
    whole=valid_end>=start+bk
    lax.fori_loop(1,jnp.where(whole,after,1),lambda i,c:(step(i,0),c)[1],0)
    lax.fori_loop(1,jnp.where(whole,1,n_off),lambda i,c:(step(i,1),c)[1],0)
    keep=(lax.broadcasted_iota(jnp.int32,(bk,W),1)<cols)
    out_ref[pl.ds(at,bk),W:2*W]=jnp.where(keep,dk_s[...],0.0).astype(BF)
    out_ref[pl.ds(at,bk),2*W:]=jnp.where(keep,dv_s[...],0.0).astype(BF)
    @pl.when(j==pl.num_programs(0)-1)
    def _():
        for c in range(0,T,512):
            x=jnp.concatenate([dq_s[:,c:c+512],jnp.zeros((W-cols,512),F32)],axis=0)
            out_ref[c:c+512,:W]=jnp.transpose(x).astype(BF)

def attn_bwd(scal,qx,packed,attn,grad,shard,nh=3,bk=512):
    T=packed.shape[0]; W=packed.shape[1]//3
    masks,fold,spread=tables(nh,W)
    return pl.pallas_call(
        functools.partial(bwd_kernel,nh,bk,shard),
        grid_spec=pltpu.PrefetchScalarGridSpec(num_scalar_prefetch=1,grid=(T//bk,),
            in_specs=[const(qx),const(packed),const(attn),const(grad),const(masks),const(fold)],
            out_specs=const(packed),
            scratch_shapes=[pltpu.VMEM((nh,T,W),BF),pltpu.VMEM((nh,T,W),BF),pltpu.VMEM((nh*HD,T),F32),
                pltpu.VMEM((bk,W),F32),pltpu.VMEM((bk,W),F32)]),
        out_shape=jax.ShapeDtypeStruct(packed.shape,BF),
        compiler_params=pltpu.CompilerParams(vmem_limit_bytes=60*2**20),
        name="attention_backward",
    )(scal,qx,packed,attn,grad,masks,fold)


EPSILON = 1e-05
TN=(((0,),(0,)),((),()))
VMEM_LIMIT=60*2**20


def widen(ref, buf):
    buf[:,:ref.shape[1]]=ref[...].astype(F32)
    lane=lax.broadcasted_iota(jnp.int32,buf.shape,1)
    return jnp.where(lane<ref.shape[1],buf[...],0.0)

def closed(x):
    lane=lax.broadcasted_iota(jnp.int32,x.shape,1)
    return jnp.where(lane<x.shape[1]-1,x,-jnp.sum(x,axis=1,keepdims=True))

def last_off(x):
    return x-x[:,x.shape[1]-1:]

def centred(x):
    return x-jnp.mean(x,axis=1,keepdims=True)

def inverse(z):
    return lax.rsqrt(jnp.mean(z*z,axis=1,keepdims=True)+EPSILON)

def norm_pull(grad,hat,inv,gain):
    dh=grad*gain
    return last_off((dh-hat*jnp.mean(dh*hat,axis=1,keepdims=True))*inv)

def first_norm_kernel(x_ref,gain_ref,n_ref,buf):
    z=closed(widen(x_ref,buf))
    n_ref[...]=(z*inverse(z)*gain_ref[...]).astype(BF)

def first_norm(stream,gain):
    T,C=stream.shape; R=min(T,256)
    return pl.pallas_call(first_norm_kernel,grid=(T//R,),
        in_specs=[pl.BlockSpec((R,C),lambda i:(i,0)),pl.BlockSpec((1,C+1),lambda i:(0,0))],
        out_specs=pl.BlockSpec((R,C+1),lambda i:(i,0)),
        out_shape=jax.ShapeDtypeStruct((T,C+1),BF),
        scratch_shapes=[pltpu.VMEM((R,C+1),F32)],name="first_norm")(stream,gain)

def last_norm_kernel(x_ref,mid_ref,own_ref,far_ref,gain_ref,out_ref,buf):
    z=closed(widen(x_ref,buf))
    inv=inverse(z)
    grad=own_ref[...].astype(F32)+far_ref[...].astype(F32)
    out=mid_ref[...]+norm_pull(grad,z*inv,inv,gain_ref[...])
    out_ref[...]=out[:,:out_ref.shape[1]]

def last_norm(stream,middle,own,far,gain):
    T,C=stream.shape; R=min(T,256)
    row=lambda w: pl.BlockSpec((R,w),lambda i:(i,0))
    return pl.pallas_call(last_norm_kernel,grid=(T//R,),
        in_specs=[row(C),row(C+1),row(C+1),row(C+1),pl.BlockSpec((1,C+1),lambda i:(0,0))],
        out_specs=row(C),out_shape=jax.ShapeDtypeStruct((T,C),F32),
        scratch_shapes=[pltpu.VMEM((R,C+1),F32)],name="last_norm")(stream,middle,own,far,gain)

def middle_kernel(n,tiles,sc_ref,x_ref,c_ref,gain_ref,*refs):
    attn=refs[:n]; weights=refs[n:2*n]
    res_ref,mid_ref,gh_ref,gw_ref,go_ref,sum_ref,buf,z_s,n_s,g_s,bm_s,gn_s=refs[2*n:]
    T,D=z_s.shape; H=attn[0].shape[1]; FD=(weights[0].shape[0]-H)//2; R=T//tiles
    k=pl.program_id(0)
    def valid_rows(r):
        span=sc_ref[1]
        at=sc_ref[16]+r*R+lax.broadcasted_iota(jnp.int32,(R,1),0)
        row=at//span
        length=jnp.zeros((R,1),jnp.int32)
        for s in range(4): length=jnp.where(row==s,sc_ref[3+s],length)
        return (row<sc_ref[2])&(at-row*span<length)
    def grad_out(r):
        buf[:,:D-1]=c_ref[r*R:(r+1)*R,:].astype(F32)
        lane=lax.broadcasted_iota(jnp.int32,(R,D),1)
        return jnp.where((lane<D-1)&valid_rows(r),buf[...],0.0)
    def squares(x,r):
        x=jnp.where(valid_rows(r),x,0.0)
        return jnp.sum((x*x).reshape(R//8,8,D),axis=0)
    @pl.when(k==0)
    def _():
        for r in range(tiles):
            at=slice(r*R,(r+1)*R)
            buf[:,:D-1]=x_ref[at,:].astype(F32)
            lane=lax.broadcasted_iota(jnp.int32,(R,D),1)
            z1=closed(jnp.where(lane<D-1,buf[...],0.0))
            ba=sum(dot(attn[s][at,:],weights[s][:H,:],NN) for s in range(n))
            z2=z1+centred(ba)
            z_s[at,:]=z2
            n_s[at,:]=(z2*inverse(z2)*gain_ref[...]).astype(BF)
            g_s[at,:]=centred(grad_out(r)).astype(BF)
            sq=squares(ba,r)
            if r==0: sum_ref[16:24,:]=sq
            else: sum_ref[16:24,:]+=sq
    def piece(s):
        w=weights[s]
        up=w[H:H+FD,:]; down=w[H+FD:,:]
        for r in range(tiles):
            at=slice(r*R,(r+1)*R)
            nr=n_s[at,:]; gr=g_s[at,:]
            x=dot(nr,up,NN)
            th=jnp.tanh(0.7978845608028654*(x+0.044715*x*x*x))
            half=0.5*(1.0+th)
            hid=(x*half).astype(BF)
            slope=half+0.5*x*(1.0-th*th)*(0.7978845608028654*(1.0+0.134145*x*x))
            gp=(dot(gr,down,NT)*slope).astype(BF)
            bm=dot(hid,down,NN); gn=dot(gp,up,NT)
            if s==0: bm_s[at,:]=bm; gn_s[at,:]=gn
            else: bm_s[at,:]+=bm; gn_s[at,:]+=gn
            gu=dot(nr,gp,TN); gd=dot(hid,gr,TN)
            if r==0: wu,wd=gu,gd
            else: wu,wd=wu+gu,wd+gd
        gw_ref[0,:FD,:]=wu.astype(BF); gw_ref[0,FD:,:]=wd.astype(BF)
    for s in range(n): pl.when(k==s)(functools.partial(piece,s))
    @pl.when(k==n-1)
    def _():
        for r in range(tiles):
            at=slice(r*R,(r+1)*R)
            z2=z_s[at,:]; inv=inverse(z2); hat=z2*inv; gn=gn_s[at,:]; bm=bm_s[at,:]
            out=z2+centred(bm)
            res_ref[at,:]=out[:,:D-1].astype(BF)
            mid=grad_out(r)+norm_pull(gn,hat,inv,gain_ref[...])
            mid_ref[at,:]=mid
            ga=centred(mid).astype(BF)
            g_s[at,:]=ga
            for s in range(n): gh_ref[s,at,:]=dot(ga,weights[s][:H,:],NT).astype(BF)
            so=squares(out,r); sm=squares(bm,r); sg=jnp.sum((gn*hat).reshape(R//8,8,D),axis=0)
            if r==0: sum_ref[0:8,:]=sg; sum_ref[8:16,:]=so; sum_ref[24:32,:]=sm
            else: sum_ref[0:8,:]+=sg; sum_ref[8:16,:]+=so; sum_ref[24:32,:]+=sm
        for s in range(n): go_ref[s]=dot(attn[s][...],g_s[...],TN).astype(BF)

def middle_part(scal,stream,cotangent,gain,attn,weights,tiles=2):
    n=len(attn); T,H=attn[0].shape; D=stream.shape[1]+1; FD=(weights[0].shape[0]-H)//2
    once=lambda a: pl.BlockSpec(a.shape,lambda i,sc:(0,)*a.ndim,pipeline_mode=pl.Buffered(1))
    whole=lambda *s: pl.BlockSpec(s,lambda i,sc:(0,)*len(s))
    return pl.pallas_call(
        functools.partial(middle_kernel,n,tiles),
        grid_spec=pltpu.PrefetchScalarGridSpec(num_scalar_prefetch=1,grid=(n,),
            in_specs=[once(stream),once(cotangent),once(gain)]+[once(a) for a in attn]+[once(w) for w in weights],
            out_specs=[whole(T,D-1),whole(T,D),whole(n,T,H),pl.BlockSpec((1,2*FD,D),lambda i,sc:(i,0,0)),whole(n,H,D),whole(32,D)],
            scratch_shapes=[pltpu.VMEM((T//tiles,D),F32),pltpu.VMEM((T,D),F32),pltpu.VMEM((T,D),BF),pltpu.VMEM((T,D),BF),pltpu.VMEM((T,D),F32),pltpu.VMEM((T,D),F32)]),
        out_shape=[jax.ShapeDtypeStruct((T,D-1),BF),jax.ShapeDtypeStruct((T,D),F32),jax.ShapeDtypeStruct((n,T,H),BF),
            jax.ShapeDtypeStruct((n,2*FD,D),BF),jax.ShapeDtypeStruct((n,H,D),BF),jax.ShapeDtypeStruct((32,D),F32)],
        compiler_params=pltpu.CompilerParams(vmem_limit_bytes=VMEM_LIMIT),
        name="middle",
    )(scal,stream,cotangent,gain,*attn,*weights)


def swap(x,axis,step):
    size=lax.axis_size(axis)
    return lax.ppermute(x,axis,[(i,i^step) for i in range(size)])

def after(x,*others):
    return lax.optimization_barrier((x,)+others)[0]

def gather_xor(x,axis):
    size=lax.axis_size(axis); got={0:x}
    step=size//2
    while step>=1:
        for have in sorted(got): got[have^step]=swap(got[have],axis,step)
        step//=2
    return [got[i] for i in range(size)]

def reduce_xor(pieces,axis):
    size=lax.axis_size(axis); step=1
    while step<size:
        keep=[i for i in sorted(pieces) if not i&step]
        sent=jnp.stack([pieces[i^step] for i in keep]) if len(keep)>1 else pieces[keep[0]^step][None]
        got=swap(sent.astype(BF),axis,step)
        if len(keep)==1: return pieces[0],got[0]
        pieces={i:pieces[i].astype(F32)+got[m].astype(F32) for m,i in enumerate(keep)}
        pieces={i:v.astype(BF) if i else v for i,v in pieces.items()}
        step*=2
    return pieces[0],None

def bit_groups(size):
    bits=[1<<b for b in range(size.bit_length()-1)]
    groups=[bits[:1]]; rest=bits[1:]
    while rest: groups.append(rest[:2]); rest=rest[2:]
    return [g for g in groups if g]

def sum_over(x,axis):
    me=lax.axis_index(axis); levels=[]
    cur=x.astype(F32)
    for bits in bit_groups(lax.axis_size(axis)):
        m=1<<len(bits); low=bits[0]
        mine=(me//low)%m
        cut=cur.reshape((m,cur.shape[0]//m)+cur.shape[1:])
        total=lax.dynamic_index_in_dim(cut,mine,0,keepdims=False)
        cutb=cut.astype(BF)
        for d in range(1,m):
            got=swap(lax.dynamic_index_in_dim(cutb,mine^d,0,keepdims=False),axis,d*low)
            total=total+got.astype(F32)
        levels.append((m,low,mine)); cur=total
    cur=cur.astype(BF)
    for m,low,mine in reversed(levels):
        full=jnp.zeros((m,)+cur.shape,BF)
        full=lax.dynamic_update_index_in_dim(full,cur,mine,0)
        for d in range(1,m):
            full=lax.dynamic_update_index_in_dim(full,swap(cur,axis,d*low),mine^d,0)
        cur=full.reshape((m*cur.shape[0],)+cur.shape[1:])
    return cur.astype(F32)

def butterfly(x,axis):
    step=1
    while step<lax.axis_size(axis):
        x=x+swap(x,axis,step); step*=2
    return x

def shards(stream,cotangent,bucket,row_counts,lengths,w_qkv,w_out,w_up,w_down,gain_one,gain_two):
    T=stream.shape[0]; D=stream.shape[1]+1; C=w_qkv.shape[2]; nh=C//HD
    n=lax.axis_size("tensor"); t=lax.axis_index("tensor")
    wide=-(-(C+4*nh)//LANES)*LANES
    span=BASE*jnp.where(bucket[0]==0,1,jnp.where(bucket[0]==1,2,4)).astype(jnp.int32)
    zero=jnp.zeros((),jnp.int32)
    scal=jnp.stack([t.astype(jnp.int32),span,row_counts[0]]+[lengths[0,r] for r in range(lengths.shape[1])]+[zero]*(13-lengths.shape[1])+[(t*T).astype(jnp.int32)])
    g1=gain_one.reshape(1,D); g2=gain_two.reshape(1,D)
    lift=np.ones((1,3,1),np.float32); lift[0,0]=HD**-0.5
    w_pad=jnp.pad(w_qkv*jnp.asarray(lift,BF),((0,0),(0,0),(0,wide-C))).reshape(D,3*wide)

    normed=first_norm(stream,g1)
    ones=gather_xor(normed,"tensor")
    gathered=jnp.concatenate(ones,axis=0)
    packed=dot(gathered,w_pad,NN).astype(BF)
    own_w=after(jnp.concatenate([w_out,w_up,w_down],axis=0),*ones)
    weights=gather_xor(own_w,"tensor")
    attn_all,qx=attn_fwd(scal,packed,T,nh)
    attn=[attn_all[:T]]+[swap(attn_all[d*T:(d+1)*T],"tensor",d) for d in range(1,n)]
    result,mid,grad_heads,gw,go,sums=middle_part(scal,stream,cotangent,g2,attn,weights)
    heads=jnp.concatenate([grad_heads[0]]+[swap(grad_heads[d],"tensor",d) for d in range(1,n)],axis=0)
    grad_packed=attn_bwd(scal,qx,packed,attn_all,heads,T,nh)

    gw,go=after(gw,go),go
    near,far=reduce_xor({i:gw[i] for i in range(n)},"tensor")
    near_o,far_o=reduce_xor({i:go[i] for i in range(n)},"tensor")
    gw_own=jnp.concatenate([near_o.astype(F32)+far_o.astype(F32),near.astype(F32)+far.astype(F32)],axis=0).astype(BF)
    gw_sum=lax.psum(gw_own,"dp").astype(F32)

    back=dot(grad_packed,w_pad,NT).astype(BF)
    own,far=reduce_xor({i:back[i*T:(i+1)*T] for i in range(n)},"tensor")
    grad_stream=last_norm(stream,mid,own,far,g1)
    gq=dot(gathered,grad_packed,TN)
    gq=gq.reshape(D,3,wide)[:,:,:C]*lift
    gain_part=jnp.sum(gq*w_qkv.astype(F32),axis=(1,2))/gain_one
    gq=sum_over(gq.reshape(D,3*C),"dp").reshape(D,3,C)
    group_tokens=jnp.sum(jnp.where(jnp.arange(lengths.shape[1])<row_counts[0],lengths[0],0)).astype(F32)/n
    s=sums.reshape(4,8,D)
    small=jnp.concatenate([gain_part,jnp.sum(s[0],axis=0),jnp.sum(s[1:],axis=(1,2)),group_tokens[None]])
    small=jnp.pad(small,(0,-small.shape[0]%LANES)).reshape(-1,LANES)
    small=butterfly(butterfly(small,"tensor"),"dp").reshape(-1)
    root=jnp.sqrt(small[2*D:2*D+3]/(D*small[2*D+3]))
    F=w_up.shape[1]
    return (result,grad_stream,gq,gw_sum[:C],gw_sum[C:C+D],gw_sum[C+D:],small[:D],small[D:2*D],root)


def solution(mesh):
    rows=P(("dp","tensor"),None)
    return jax.shard_map(shards,mesh=mesh,
        in_specs=(rows,rows,P("dp"),P("dp"),P("dp",None),P(None,None,"tensor"),P("tensor",None),P(None,"tensor"),P("tensor",None),P(),P()),
        out_specs=(rows,rows,P(None,None,"tensor"),P("tensor",None),P(None,"tensor"),P("tensor",None),P(),P(),P()),
        check_vma=False)
```

```python
import functools
import jax, jax.numpy as jnp, numpy as np
from jax import lax
from jax.experimental import pallas as pl
from jax.experimental.pallas import tpu as pltpu
from jax.sharding import PartitionSpec as P
HD=64; BASE=1024
LANES=128
SHIFT_LIMIT=70.0
F32=jnp.float32; BF=jnp.bfloat16
NT=(((1,),(1,)),((),()))
NN=(((1,),(0,)),((),()))
def dot(a,b,dims): return lax.dot_general(a,b,dims,preferred_element_type=F32)

def tables(nh, wide):
    cols=nh*HD; lane=np.arange(wide)
    head=np.where(lane<cols,lane//HD,np.where(lane<cols+4*nh,(lane-cols)//4,-1))
    spare=(lane>=cols)&(lane<cols+4*nh)
    masks=np.zeros((8,wide),np.float32)
    for h in range(nh): masks[h]=(head==h)
    masks[nh]=spare
    for h in range(nh): masks[nh+1+h]=spare&(head==h)
    fold=np.zeros((wide,LANES),np.float32)
    hi=wide-LANES
    same=(head[:,None]==head[None,hi:])&(head[:,None]>=0)
    fold[:]=same&(lane<cols)[:,None]&spare[None,hi:]
    spread=np.zeros((LANES,wide),np.float32)
    spread[:]=(same&(lane<cols)[:,None]&spare[None,hi:]).T
    return jnp.asarray(masks,BF),jnp.asarray(fold,BF),jnp.asarray(spread,BF)

def row_info(sc_ref, start):
    span=sc_ref[1]
    row=start//span
    length=sc_ref[3]
    for r in range(1,4):
        length=jnp.where(row==r, sc_ref[3+r], length)
    length=jnp.where(row<sc_ref[2], length, 0)
    return row*span, row*span+length, row*span+span

def place(sc_ref, start, shard):
    return pl.multiple_of((jnp.bitwise_xor(start//shard, sc_ref[0]))*shard + start%shard, 256)

def parts(x, cols, hi):
    lane=lax.broadcasted_iota(jnp.int32,x.shape,1)+hi-cols
    which=jnp.where(lane<0,3,lane%4)
    a=x.astype(BF).astype(F32); r=x-a; b=r.astype(BF).astype(F32); c=r-b
    return jnp.where(which==0,a,jnp.where(which==1,b,jnp.where(which==2,c,0.0))).astype(BF)

def fwd_kernel(nh, bq, shard, sc_ref, p_ref, mask_ref, fold_ref, spread_ref, *refs):
    n=p_ref.shape[0]//shard; o_refs=refs[:n]; qx_ref, q_s, k_s, v_s, kn_s, sh_s, a_s=refs[n:]
    T=p_ref.shape[0]; W=p_ref.shape[1]//3; hi=W-LANES; cols=nh*HD
    i=pl.program_id(0)
    @pl.when(i==0)
    def _():
        kn=jnp.zeros((8,LANES),F32)
        for c in range(0,T,512):
            k=p_ref[c:c+512,W:2*W]; v=p_ref[c:c+512,2*W:]
            k_s[c:c+512,:]=k+mask_ref[nh:nh+1,:]
            kn=jnp.maximum(kn,jnp.max(dot(k*k,fold_ref[...],NN).reshape(64,8,LANES),axis=0))
            for h in range(nh):
                v_s[h,c:c+512,:]=v*mask_ref[h:h+1,:]+mask_ref[nh+1+h:nh+2+h,:]
        kn_s[...]=jnp.broadcast_to(jnp.max(kn,axis=0,keepdims=True),(8,LANES))
    start=i*bq
    row_start,valid_end,_=row_info(sc_ref,start)
    at=place(sc_ref,start,shard)
    q=p_ref[pl.ds(at,bq),:W]; own=p_ref[pl.ds(at,bq),W:2*W]
    before=(start-row_start)//bq
    full=jnp.minimum(before,(valid_end-row_start)//bq)
    some=jnp.minimum(before,(valid_end-row_start+bq-1)//bq)
    rows=lax.broadcasted_iota(jnp.int32,(bq,bq),0); tcol=lax.broadcasted_iota(jnp.int32,(bq,bq),1)
    diag=(tcol==rows)|((tcol<rows)&(tcol<valid_end-start))
    def set_q(shift_lanes):
        x=jnp.concatenate([q[:,:hi],q[:,hi:]+shift_lanes],axis=1)
        for h in range(nh): q_s[h]=x*mask_ref[h:h+1,:]
    self_score=dot(q*own,fold_ref[...],NN)
    shift=self_score.astype(BF).astype(F32)
    sh_s[...]=shift
    set_q(parts(-shift,cols,hi))
    size=jnp.sqrt(dot(q*q,fold_ref[...],NN)*kn_s[:1,:])*1.02
    bounded=jnp.max(size-shift)<=SHIFT_LIMIT
    @pl.when(jnp.logical_not(bounded))
    def _():
        lane=lax.broadcasted_iota(jnp.int32,(bq,LANES),1)+hi-cols
        new=jnp.zeros((bq,LANES),F32)
        for h in range(nh):
            qh=q*mask_ref[h:h+1,:]
            m0=jnp.max(jnp.where(diag,dot(qh,k_s[pl.ds(at,bq),:],NT),-1e30),axis=1,keepdims=True)
            def look(j,m):
                b=row_start+j*bq
                s=dot(qh,k_s[pl.ds(place(sc_ref,b,shard),bq),:],NT)
                s=jnp.where(tcol<valid_end-b,s,-1e30)
                return jnp.maximum(m,jnp.max(s,axis=1,keepdims=True))
            m=lax.fori_loop(0,some,look,m0)
            new=jnp.where((lane>=4*h)&(lane<4*h+4),m,new)
        sh_s[...]=new
        set_q(parts(-new,cols,hi))
    def step(b,masking,first):
        bt=place(sc_ref,b,shard)
        k=k_s[pl.ds(bt,bq),:]
        ps=[]
        for h in range(nh):
            s=dot(q_s[h],k,NT)
            if masking is not None: s=jnp.where(masking,s,-1e30)
            ps.append(jnp.exp(s).astype(BF))
        new=dot(jnp.concatenate(ps,axis=1),v_s[:,pl.ds(bt,bq),:].reshape(nh*bq,W),NN)
        if first: a_s[...]=new
        else: a_s[...]+=new
    step(start,diag,True)
    def whole(j,c):
        step(row_start+j*bq,None,False); return c
    def partly(j,c):
        b=row_start+j*bq
        step(b,tcol<valid_end-b,False); return c
    lax.fori_loop(0,full,whole,0)
    lax.fori_loop(full,some,partly,0)
    total=a_s[:,hi:]
    lane=lax.broadcasted_iota(jnp.int32,(bq,LANES),1)+hi-cols
    spare=(lane>=0)&(lane<4*nh)
    total=jnp.where(spare,total,1.0)
    out=(a_s[:,:cols]*dot(parts(1.0/total,cols,hi),spread_ref[...],NN)[:,:cols]).astype(BF)
    for s in range(n):
        @pl.when(at//shard==s)
        def _(): o_refs[s][pl.ds(pl.multiple_of(at%shard,bq),bq),:]=out
    lse=jnp.where(spare,sh_s[...]+jnp.log(total),0.0)
    qx_ref[...]=jnp.concatenate([q[:,:hi],q[:,hi:]+parts(-lse,cols,hi)],axis=1)

def const(a): return pl.BlockSpec(a.shape,lambda i,sc:(0,)*a.ndim)

def attn_fwd(scal, packed, shard, nh=3, bq=512):
    T=packed.shape[0]; W=packed.shape[1]//3
    tabs=tables(nh,W)
    def where(i,sc):
        per=shard//bq
        return (jnp.bitwise_xor(i//per,sc[0])*per+i%per,0)
    return pl.pallas_call(
        functools.partial(fwd_kernel,nh,bq,shard),
        grid_spec=pltpu.PrefetchScalarGridSpec(num_scalar_prefetch=1,grid=(T//bq,),
            in_specs=[once(packed)]+[once(a) for a in tabs],
            out_specs=[pl.BlockSpec((shard,nh*HD),lambda i,sc:(0,0))]*(T//shard)+[pl.BlockSpec((bq,W),where)],
            scratch_shapes=[pltpu.VMEM((nh,bq,W),BF),pltpu.VMEM((T,W),BF),pltpu.VMEM((nh,T,W),BF),
                pltpu.VMEM((8,LANES),F32),pltpu.VMEM((bq,LANES),F32),pltpu.VMEM((bq,W),F32)]),
        out_shape=[jax.ShapeDtypeStruct((shard,nh*HD),BF)]*(T//shard)+[jax.ShapeDtypeStruct((T,W),BF)],
        compiler_params=pltpu.CompilerParams(vmem_limit_bytes=56*2**20),
        name="attention_forward",
    )(scal,packed,*tabs)

def bwd_kernel(nh,heads,n,bk,shard,sc_ref,qx_ref,p_ref,*refs):
    o_refs=refs[:n]; g_refs=refs[n:2*n]; mask_ref,fold_ref=refs[2*n:2*n+2]
    old_ref=refs[2*n+2] if len(refs)>2*n+8 else None
    out_ref,q_s,d_s,dq_s,dk_s,dv_s=refs[-6:]; m=len(heads)
    T=p_ref.shape[0]; W=p_ref.shape[1]//3; hi=W-LANES; cols=nh*HD
    j=pl.program_id(0)
    @pl.when(j==0)
    def _():
        for c in range(0,T,512):
            qx=qx_ref[c:c+512,:]
            g=g_refs[c//shard][c%shard:c%shard+512,:]
            og=o_refs[c//shard][c%shard:c%shard+512,:].astype(F32)*g.astype(F32)
            og1=og.astype(BF); og2=(og-og1.astype(F32)).astype(BF)
            delta=dot(og1,fold_ref[:cols,:],NN)+dot(og2,fold_ref[:cols,:],NN)
            gx=jnp.concatenate([g,jnp.zeros((512,W-cols),BF)],axis=1)
            gx=jnp.concatenate([gx[:,:hi],gx[:,hi:]+parts(-delta,cols,hi)],axis=1)
            for i,h in enumerate(heads):
                q_s[i,c:c+512,:]=qx*mask_ref[h:h+1,:]
                d_s[i,c:c+512,:]=gx*mask_ref[h:h+1,:]
            dq_s[:,c:c+512]=jnp.zeros((m*HD,512),F32)
    start=j*bk
    row_start,valid_end,row_end=row_info(sc_ref,start)
    at=place(sc_ref,start,shard)
    k0=p_ref[pl.ds(at,bk),W:2*W]
    k=k0+mask_ref[nh:nh+1,:]; v=p_ref[pl.ds(at,bk),2*W:]+mask_ref[nh:nh+1,:]
    kt=jnp.transpose(k0)
    def step(i,kind):
        b=start+i*bk
        bt=place(sc_ref,b,shard)
        if kind!=0:
            krow=lax.broadcasted_iota(jnp.int32,(bk,bk),0); qcol=lax.broadcasted_iota(jnp.int32,(bk,bk),1)
            ok=krow<valid_end-start
            if kind==2: ok=(krow==qcol)|((krow<qcol)&ok)
        ps=[];dss=[]
        for i,h in enumerate(heads):
            s=dot(k,q_s[i,pl.ds(bt,bk),:],NT)
            if kind!=0: s=jnp.where(ok,s,-1e30)
            p=jnp.exp(s)
            ds=(p*dot(v,d_s[i,pl.ds(bt,bk),:],NT)).astype(BF)
            ps.append(p.astype(BF)); dss.append(ds)
            dq_s[i*HD:(i+1)*HD,pl.ds(bt,bk)]+=dot(kt[h*HD:(h+1)*HD],ds,NN)
        dv=dot(jnp.concatenate(ps,axis=1),d_s[:,pl.ds(bt,bk),:].reshape(m*bk,W),NN)
        dk=dot(jnp.concatenate(dss,axis=1),q_s[:,pl.ds(bt,bk),:].reshape(m*bk,W),NN)
        if kind==2: dv_s[...]=dv; dk_s[...]=dk
        else: dv_s[...]+=dv; dk_s[...]+=dk
    after=(row_end-start)//bk
    n_off=jnp.where(valid_end>start,after,1)
    step(0,2)
    whole=valid_end>=start+bk
    lax.fori_loop(1,jnp.where(whole,after,1),lambda i,c:(step(i,0),c)[1],0)
    lax.fori_loop(1,jnp.where(whole,1,n_off),lambda i,c:(step(i,1),c)[1],0)
    keep=(lax.broadcasted_iota(jnp.int32,(bk,W),1)<cols)
    def put(rows,at_lane,x):
        x=x.astype(BF)
        if old_ref is not None: x=x+old_ref[rows,at_lane:at_lane+W]
        out_ref[rows,at_lane:at_lane+W]=x
    put(pl.ds(at,bk),W,jnp.where(keep,dk_s[...],0.0))
    put(pl.ds(at,bk),2*W,jnp.where(keep,dv_s[...],0.0))
    @pl.when(j==pl.num_programs(0)-1)
    def _():
        for c in range(0,T,512):
            first=heads[0]*HD; rest=W-first-m*HD
            x=dq_s[:,c:c+512]
            if first: x=jnp.concatenate([jnp.zeros((first,512),F32),x],axis=0)
            if rest: x=jnp.concatenate([x,jnp.zeros((rest,512),F32)],axis=0)
            put(slice(c,c+512),0,jnp.transpose(x))

def once(a): return pl.BlockSpec(a.shape,lambda i,sc:(0,)*a.ndim,pipeline_mode=pl.Buffered(1))

def attn_bwd(scal,qx,packed,attn,grads,shard,nh,heads,old=None,bk=512):
    T=packed.shape[0]; W=packed.shape[1]//3; m=len(heads)
    masks,fold,spread=tables(nh,W)
    more=[] if old is None else [old]
    args=[qx,packed,*attn,*grads,masks,fold]+more
    return pl.pallas_call(
        functools.partial(bwd_kernel,nh,heads,len(grads),bk,shard),
        grid_spec=pltpu.PrefetchScalarGridSpec(num_scalar_prefetch=1,grid=(T//bk,),
            in_specs=[once(x) for x in args],
            out_specs=const(packed),
            scratch_shapes=[pltpu.VMEM((m,T,W),BF),pltpu.VMEM((m,T,W),BF),pltpu.VMEM((m*HD,T),F32),
                pltpu.VMEM((bk,W),F32),pltpu.VMEM((bk,W),F32)]),
        out_shape=jax.ShapeDtypeStruct(packed.shape,BF),
        compiler_params=pltpu.CompilerParams(vmem_limit_bytes=60*2**20),
        name="attention_backward",
    )(scal,*args)


EPSILON = 1e-05
TN=(((0,),(0,)),((),()))
VMEM_LIMIT=60*2**20


def widen(ref, buf):
    buf[:,:ref.shape[1]]=ref[...].astype(F32)
    lane=lax.broadcasted_iota(jnp.int32,buf.shape,1)
    return jnp.where(lane<ref.shape[1],buf[...],0.0)

def closed(x):
    lane=lax.broadcasted_iota(jnp.int32,x.shape,1)
    return jnp.where(lane<x.shape[1]-1,x,-jnp.sum(x,axis=1,keepdims=True))

def last_off(x):
    return x-x[:,x.shape[1]-1:]

def centred(x):
    return x-jnp.mean(x,axis=1,keepdims=True)

def inverse(z):
    return lax.rsqrt(jnp.mean(z*z,axis=1,keepdims=True)+EPSILON)

def norm_pull(grad,hat,inv,gain):
    dh=grad*gain
    return last_off((dh-hat*jnp.mean(dh*hat,axis=1,keepdims=True))*inv)

def first_norm_kernel(x_ref,gain_ref,n_ref,buf):
    z=closed(widen(x_ref,buf))
    n_ref[...]=(z*inverse(z)*gain_ref[...]).astype(BF)

def first_norm(stream,gain):
    T,C=stream.shape; R=min(T,256)
    return pl.pallas_call(first_norm_kernel,grid=(T//R,),
        in_specs=[pl.BlockSpec((R,C),lambda i:(i,0)),pl.BlockSpec((1,C+1),lambda i:(0,0))],
        out_specs=pl.BlockSpec((R,C+1),lambda i:(i,0)),
        out_shape=jax.ShapeDtypeStruct((T,C+1),BF),
        scratch_shapes=[pltpu.VMEM((R,C+1),F32)],name="first_norm")(stream,gain)

def project_kernel(sc_ref,x_ref,y_ref,w_ref,*refs):
    out_ref=refs[-1]
    @pl.when(pl.program_id(0)==0)
    def _(): out_ref[...]=dot(x_ref[...],w_ref[...],NN).astype(BF)
    @pl.when(pl.program_id(0)==1)
    def _(): out_ref[...]=dot(y_ref[...],w_ref[...],NN).astype(BF)

def project(scal,x,y,w,count,at,old=None):
    T,D=x.shape; N=w.shape[1]
    more=[] if old is None else [old]
    return pl.pallas_call(project_kernel,
        grid_spec=pltpu.PrefetchScalarGridSpec(num_scalar_prefetch=1,grid=(2,),
            in_specs=[const(x),const(y),const(w)]+[pl.BlockSpec(memory_space=pl.ANY)]*len(more),
            out_specs=pl.BlockSpec((T,N),lambda i,sc:(at+i,0))),
        out_shape=jax.ShapeDtypeStruct((count*T,N),BF),
        input_output_aliases={4:0} if more else {},
        compiler_params=pltpu.CompilerParams(vmem_limit_bytes=VMEM_LIMIT),
        name="project")(scal,x,y,w,*more)

def last_norm_kernel(x_ref,mid_ref,a_ref,b_ref,c_ref,gain_ref,out_ref,buf):
    z=closed(widen(x_ref,buf))
    inv=inverse(z)
    grad=(a_ref[...].astype(F32)+b_ref[...].astype(F32))+c_ref[...].astype(F32)
    out=mid_ref[...]+norm_pull(grad,z*inv,inv,gain_ref[...])
    out_ref[...]=out[:,:out_ref.shape[1]]

def last_norm(stream,middle,terms,gain):
    T,C=stream.shape; R=min(T,256)
    row=lambda w: pl.BlockSpec((R,w),lambda i:(i,0))
    return pl.pallas_call(last_norm_kernel,grid=(T//R,),
        in_specs=[row(C)]+[row(C+1)]*4+[pl.BlockSpec((1,C+1),lambda i:(0,0))],
        out_specs=row(C),out_shape=jax.ShapeDtypeStruct((T,C),F32),
        scratch_shapes=[pltpu.VMEM((R,C+1),F32)],name="last_norm")(stream,middle,*terms,gain)

def piece_order(n):
    return [i for i in range(n) if i&1]+[i for i in range(n) if not i&1]

def middle_kernel(n,R,sc_ref,x_ref,c_ref,gain_ref,*refs):
    attn=refs[:n]; outw=refs[n:2*n]; weights=refs[2*n:3*n]; gh=refs[3*n:4*n]
    res_ref,mid_ref,send_ref,keep_ref,go_ref,sum_ref,buf,z_s,n_s,g_s,bm_s,gn_s,w_s,wu_s,wd_s,sem=refs[4*n:]
    T,D=z_s.shape; H=attn[0].shape[1]; FD=w_s.shape[1]//2; tiles=T//R
    k=pl.program_id(0); order=piece_order(n)
    lane=lax.broadcasted_iota(jnp.int32,(R,D),1)
    def fetch(s,slot): return pltpu.make_async_copy(weights[s].at[H:,:],w_s.at[slot],sem.at[slot])
    def rows(r): return pl.ds(pl.multiple_of(r*R,R),R)
    def valid_rows(r):
        start=sc_ref[16]+r*R
        return lax.broadcasted_iota(jnp.int32,(R,D),0)<row_info(sc_ref,start)[1]-start
    def grad_out(r):
        buf[:,:D-1]=c_ref[rows(r),:].astype(F32)
        return jnp.where((lane<D-1)&valid_rows(r),buf[...],0.0)
    def squares(x,r):
        x=jnp.where(valid_rows(r),x,0.0)
        return jnp.sum((x*x).reshape(R//8,8,D),axis=0)
    @pl.when(k==0)
    def _():
        fetch(order[0],0).start()
        sum_ref[...]=jnp.zeros_like(sum_ref)
        def first(r,carry):
            at=rows(r)
            buf[:,:D-1]=x_ref[at,:].astype(F32)
            z1=closed(jnp.where(lane<D-1,buf[...],0.0))
            ba=sum(dot(attn[s][at,:],outw[s][...],NN) for s in range(n))
            z2=z1+centred(ba)
            z_s[at,:]=z2
            n_s[at,:]=(z2*inverse(z2)*gain_ref[...]).astype(BF)
            g_s[at,:]=centred(grad_out(r)).astype(BF)
            bm_s[at,:]=jnp.zeros((R,D),F32); gn_s[at,:]=jnp.zeros((R,D),F32)
            sum_ref[16:24,:]+=squares(ba,r)
            return carry
        lax.fori_loop(0,tiles,first,0)
    slot=k%2
    for s in range(n):
        @pl.when(k==s)
        def _():
            fetch(order[s],s%2).wait()
            if s+1<n: fetch(order[s+1],(s+1)%2).start()
    def piece(r,carry):
        at=rows(r)
        nr=n_s[at,:]; gr=g_s[at,:]
        up=w_s[slot,:FD,:]; down=w_s[slot,FD:,:]
        x=dot(nr,up,NN)
        sq=x*x
        th=jnp.tanh(x*(0.7978845608028654+0.035677408136300125*sq))
        half=0.5+0.5*th
        hid=(x*half).astype(BF)
        slope=half+0.5*x*(1.0-th*th)*(0.7978845608028654+0.10703222440890037*sq)
        gp=(dot(gr,down,NT)*slope).astype(BF)
        bm_s[at,:]+=dot(hid,down,NN); gn_s[at,:]+=dot(gp,up,NT)
        wu_s[...]+=dot(nr,gp,TN); wd_s[...]+=dot(hid,gr,TN)
        return carry
    wu_s[...]=jnp.zeros_like(wu_s); wd_s[...]=jnp.zeros_like(wd_s)
    lax.fori_loop(0,tiles,piece,0)
    def put(ref):
        ref[0,:FD,:]=wu_s[...].astype(BF); ref[0,FD:,:]=wd_s[...].astype(BF)
    pl.when(k<n//2)(functools.partial(put,send_ref))
    pl.when(k>=n//2)(functools.partial(put,keep_ref))
    @pl.when(k==n-1)
    def _():
        def final(r,carry):
            at=rows(r)
            z2=z_s[at,:]; inv=inverse(z2); hat=z2*inv; gn=gn_s[at,:]; bm=bm_s[at,:]
            out=z2+centred(bm)
            res_ref[at,:]=out[:,:D-1].astype(BF)
            mid=grad_out(r)+norm_pull(gn,hat,inv,gain_ref[...])
            mid_ref[at,:]=mid
            ga=centred(mid).astype(BF)
            g_s[at,:]=ga
            for s in range(n): gh[s][at,:]=dot(ga,outw[s][...],NT).astype(BF)
            sum_ref[0:8,:]+=jnp.sum((gn*hat).reshape(R//8,8,D),axis=0)
            sum_ref[8:16,:]+=squares(out,r); sum_ref[24:32,:]+=squares(bm,r)
            return carry
        lax.fori_loop(0,tiles,final,0)
        for s in range(n): go_ref[s]=dot(attn[order[s]][...],g_s[...],TN).astype(BF)

def middle_part(scal,stream,cotangent,gain,attn,weights,R=256):
    n=len(attn); T,H=attn[0].shape; D=stream.shape[1]+1; FD=(weights[0].shape[0]-H)//2; R=min(R,T)
    once=lambda a: pl.BlockSpec(a.shape,lambda i,sc:(0,)*a.ndim,pipeline_mode=pl.Buffered(1))
    whole=lambda *s: pl.BlockSpec(s,lambda i,sc:(0,)*len(s))
    top=pl.BlockSpec((H,D),lambda i,sc:(0,0),pipeline_mode=pl.Buffered(1))
    return pl.pallas_call(
        functools.partial(middle_kernel,n,R),
        grid_spec=pltpu.PrefetchScalarGridSpec(num_scalar_prefetch=1,grid=(n,),
            in_specs=[once(stream),once(cotangent),once(gain)]+[once(a) for a in attn]+[top]*n+[pl.BlockSpec(memory_space=pl.ANY)]*n,
            out_specs=[whole(T,H)]*n+[whole(T,D-1),whole(T,D),pl.BlockSpec((1,2*FD,D),lambda i,sc:(jnp.minimum(i,n//2-1),0,0)),
                pl.BlockSpec((1,2*FD,D),lambda i,sc:(jnp.maximum(i-n//2,0),0,0)),whole(n,H,D),whole(32,D)],
            scratch_shapes=[pltpu.VMEM((R,D),F32),pltpu.VMEM((T,D),F32),pltpu.VMEM((T,D),BF),pltpu.VMEM((T,D),BF),pltpu.VMEM((T,D),F32),pltpu.VMEM((T,D),F32),
                pltpu.VMEM((2,2*FD,D),BF),pltpu.VMEM((D,FD),F32),pltpu.VMEM((FD,D),F32),pltpu.SemaphoreType.DMA((2,))]),
        out_shape=[jax.ShapeDtypeStruct((T,H),BF)]*n+[jax.ShapeDtypeStruct((T,D-1),BF),jax.ShapeDtypeStruct((T,D),F32),
            jax.ShapeDtypeStruct((n//2,2*FD,D),BF),jax.ShapeDtypeStruct((n//2,2*FD,D),BF),jax.ShapeDtypeStruct((n,H,D),BF),jax.ShapeDtypeStruct((32,D),F32)],
        compiler_params=pltpu.CompilerParams(vmem_limit_bytes=VMEM_LIMIT),
        name="middle",
    )(scal,stream,cotangent,gain,*attn,*weights,*weights)


def swap(x,axis,step):
    size=lax.axis_size(axis)
    return lax.ppermute(x,axis,[(i,i^step) for i in range(size)])

def after(x,*others):
    return lax.optimization_barrier((x,)+others)[0]

def choose(options,index):
    out=options[0]
    for i in range(1,len(options)): out=jnp.where(index==i,options[i],out)
    return out

def bit_groups(size):
    bits=[1<<b for b in range(size.bit_length()-1)]
    groups=[bits[:1]]; rest=bits[1:]
    while rest: groups.append(rest[:2]); rest=rest[2:]
    return [g for g in groups if g]

def sum_over(x,axis,first):
    me=lax.axis_index(axis); levels=[]
    cur=x
    for bits in bit_groups(lax.axis_size(axis)):
        m=1<<len(bits); low=bits[0]
        mine=(me//low)%m
        rows=cur.shape[0]//m
        cut=[cur[i*rows:(i+1)*rows] for i in range(m)]
        total=choose(cut,mine)
        for d in range(1,m):
            total=total+swap(choose([cut[i^d] for i in range(m)],mine).astype(BF),axis,d*low).astype(F32)
        levels.append((m,low,mine)); cur=total
    cur,first=lax.optimization_barrier((cur.astype(BF),first))
    for m,low,mine in reversed(levels):
        got=[cur]+[swap(cur,axis,d*low) for d in range(1,m)]
        cur=jnp.concatenate([choose([got[i^p] for i in range(m)],mine) for p in range(m)],axis=0)
    return cur.astype(F32),first

def butterfly(x,axis):
    step=1
    while step<lax.axis_size(axis):
        x=x+swap(x,axis,step); step*=2
    return x

def shards(stream,cotangent,bucket,row_counts,lengths,w_qkv,w_out,w_up,w_down,gain_one,gain_two):
    T=stream.shape[0]; D=stream.shape[1]+1; C=w_qkv.shape[2]; nh=C//HD
    n=lax.axis_size("tensor"); t=lax.axis_index("tensor")
    wide=-(-(C+4*nh)//LANES)*LANES
    span=BASE*jnp.where(bucket[0]==0,1,jnp.where(bucket[0]==1,2,4)).astype(jnp.int32)
    zero=jnp.zeros((),jnp.int32)
    scal=jnp.stack([t.astype(jnp.int32),span,row_counts[0]]+[lengths[0,r] for r in range(lengths.shape[1])]+[zero]*(13-lengths.shape[1])+[(t*T).astype(jnp.int32)])
    g1=gain_one.reshape(1,D); g2=gain_two.reshape(1,D)
    lift=np.ones((1,3,1),np.float32); lift[0,0]=HD**-0.5
    w_pad=jnp.pad(w_qkv*jnp.asarray(lift,BF),((0,0),(0,0),(0,wide-C))).reshape(D,3*wide)

    normed=first_norm(stream,g1)
    far=swap(normed,"tensor",2); near=swap(normed,"tensor",1)
    own_w=after(jnp.concatenate([w_out,w_up,w_down],axis=0),far)
    far_w=swap(own_w,"tensor",2); near_w=swap(own_w,"tensor",1)
    corner=swap(far,"tensor",1)
    packed=project(scal,normed,near,w_pad,n,0)
    packed=project(scal,far,corner,w_pad,n,2,packed)
    *heads_out,qx=attn_fwd(scal,packed,T,nh)
    attn=[heads_out[0]]+[swap(heads_out[d],"tensor",d) for d in range(1,n)]
    weights=[own_w,near_w,far_w,swap(after(far_w,attn[1]),"tensor",1)]
    *grad_heads,result,mid,w_send,w_keep,go,sums=middle_part(scal,stream,cotangent,g2,attn,weights)
    heads=[grad_heads[0]]+[swap(grad_heads[d],"tensor",d) for d in range(1,n)]
    w_send,go_send=lax.optimization_barrier((w_send,go[:n//2],heads[1]))[:2]
    w_got=swap(w_send,"tensor",1); o_got=swap(go_send,"tensor",1)
    R=C+w_keep.shape[1]; q=lax.axis_size("dp"); r=R//q
    flat=lambda x: x.reshape(q,-1,D)
    w_half=(w_keep.astype(F32)+w_got.astype(F32)).astype(BF); o_half=(go[n//2:].astype(F32)+o_got.astype(F32)).astype(BF)
    w_half=jnp.concatenate([flat(x) for i in range(2) for x in (o_half[i],w_half[i,:D],w_half[i,D:])],axis=1).reshape(2*R,D)
    w_part=lax.psum_scatter(w_half,"dp",scatter_dimension=0,tiled=True)

    grad_packed=attn_bwd(scal,qx,packed,heads_out,heads,T,nh,list(range(nh)))
    back={i:dot(grad_packed[i*T:(i+1)*T],w_pad,NT).astype(BF) for i in piece_order(n)}
    near_b={i:swap(back[i^1],"tensor",1) for i in (0,2)}
    two=(back[2].astype(F32)+near_b[2].astype(F32)).astype(BF)
    far_b=swap(two,"tensor",2)
    gathered=jnp.concatenate([normed,near,far,corner],axis=0)
    gq=dot(gathered,after(grad_packed,two),TN)
    gq=gq.reshape(D,3,wide)[:,:,:C]*lift
    gain_part=jnp.sum(gq*w_qkv.astype(F32),axis=(1,2))/gain_one
    w_other=swap(w_part[r:],"tensor",2)
    w_own=(w_part[:r].astype(F32)+w_other.astype(F32)).astype(BF)
    w_sum=lax.all_gather(w_own,"dp",axis=0).astype(F32)
    grad_stream=last_norm(stream,mid,[back[0],near_b[0],far_b],g1)
    gq,grad_stream=sum_over(gq.reshape(D,3*C),"dp",grad_stream)
    gq=gq.reshape(D,3,C)
    cut=[0]
    for part in (C,D,w_keep.shape[1]-D): cut.append(cut[-1]+part//q)
    g_out,g_up,g_down=[w_sum[:,i:j].reshape(-1,D) for i,j in zip(cut[:-1],cut[1:])]
    group_tokens=jnp.sum(jnp.where(jnp.arange(lengths.shape[1])<row_counts[0],lengths[0],0)).astype(F32)/n
    s=sums.reshape(4,8,D)
    small=jnp.concatenate([gain_part,jnp.sum(s[0],axis=0),jnp.sum(s[1:],axis=(1,2)),group_tokens[None]])
    small=jnp.pad(small,(0,-small.shape[0]%LANES)).reshape(-1,LANES)
    small=butterfly(butterfly(small,"tensor"),"dp").reshape(-1)
    root=jnp.sqrt(small[2*D:2*D+3]/(D*small[2*D+3]))
    return (result,grad_stream,gq,g_out,g_up,g_down,small[:D],small[D:2*D],root)


def solution(mesh):
    rows=P(("dp","tensor"),None)
    return jax.shard_map(shards,mesh=mesh,
        in_specs=(rows,rows,P("dp"),P("dp"),P("dp",None),P(None,None,"tensor"),P("tensor",None),P(None,"tensor"),P("tensor",None),P(),P()),
        out_specs=(rows,rows,P(None,None,"tensor"),P("tensor",None),P(None,"tensor"),P("tensor",None),P(),P(),P()),
        check_vma=False)
```

```python
import functools
import jax, jax.numpy as jnp, numpy as np
from jax import lax
from jax.experimental import pallas as pl
from jax.experimental.pallas import tpu as pltpu
from jax.sharding import PartitionSpec as P
HD=64; BASE=1024
LANES=128
SHIFT_LIMIT=70.0
F32=jnp.float32; BF=jnp.bfloat16
NT=(((1,),(1,)),((),()))
NN=(((1,),(0,)),((),()))
def dot(a,b,dims): return lax.dot_general(a,b,dims,preferred_element_type=F32)

def tables(nh, wide):
    cols=nh*HD; lane=np.arange(wide)
    head=np.where(lane<cols,lane//HD,np.where(lane<cols+4*nh,(lane-cols)//4,-1))
    spare=(lane>=cols)&(lane<cols+4*nh)
    masks=np.zeros((8,wide),np.float32)
    for h in range(nh): masks[h]=(head==h)
    masks[nh]=spare
    for h in range(nh): masks[nh+1+h]=spare&(head==h)
    fold=np.zeros((wide,LANES),np.float32)
    hi=wide-LANES
    same=(head[:,None]==head[None,hi:])&(head[:,None]>=0)
    fold[:]=same&(lane<cols)[:,None]&spare[None,hi:]
    spread=np.zeros((LANES,wide),np.float32)
    spread[:]=(same&(lane<cols)[:,None]&spare[None,hi:]).T
    return jnp.asarray(masks,BF),jnp.asarray(fold,BF),jnp.asarray(spread,BF)

def row_info(sc_ref, start):
    span=sc_ref[1]
    row=start//span
    length=sc_ref[3]
    for r in range(1,4):
        length=jnp.where(row==r, sc_ref[3+r], length)
    length=jnp.where(row<sc_ref[2], length, 0)
    return row*span, row*span+length, row*span+span

def place(sc_ref, start, shard):
    return pl.multiple_of((jnp.bitwise_xor(start//shard, sc_ref[0]))*shard + start%shard, 256)

def parts(x, cols, hi):
    lane=lax.broadcasted_iota(jnp.int32,x.shape,1)+hi-cols
    which=jnp.where(lane<0,3,lane%4)
    a=x.astype(BF).astype(F32); r=x-a; b=r.astype(BF).astype(F32); c=r-b
    return jnp.where(which==0,a,jnp.where(which==1,b,jnp.where(which==2,c,0.0))).astype(BF)

def fwd_kernel(nh, bq, shard, sc_ref, p_ref, mask_ref, fold_ref, spread_ref, *refs):
    n=p_ref.shape[0]//shard; o_refs=refs[:n]; qx_ref, q_s, k_s, v_s, kn_s, sh_s, a_s=refs[n:]
    T=p_ref.shape[0]; W=p_ref.shape[1]//3; hi=W-LANES; cols=nh*HD
    i=pl.program_id(0)
    @pl.when(i==0)
    def _():
        kn=jnp.zeros((8,LANES),F32)
        for c in range(0,T,512):
            k=p_ref[c:c+512,W:2*W]; v=p_ref[c:c+512,2*W:]
            k_s[c:c+512,:]=k+mask_ref[nh:nh+1,:]
            kn=jnp.maximum(kn,jnp.max(dot(k*k,fold_ref[...],NN).reshape(64,8,LANES),axis=0))
            for h in range(nh):
                v_s[h,c:c+512,:]=v*mask_ref[h:h+1,:]+mask_ref[nh+1+h:nh+2+h,:]
        kn_s[...]=jnp.broadcast_to(jnp.max(kn,axis=0,keepdims=True),(8,LANES))
    start=i*bq
    row_start,valid_end,_=row_info(sc_ref,start)
    at=place(sc_ref,start,shard)
    q=p_ref[pl.ds(at,bq),:W]; own=p_ref[pl.ds(at,bq),W:2*W]
    before=(start-row_start)//bq
    full=jnp.minimum(before,(valid_end-row_start)//bq)
    some=jnp.minimum(before,(valid_end-row_start+bq-1)//bq)
    rows=lax.broadcasted_iota(jnp.int32,(bq,bq),0); tcol=lax.broadcasted_iota(jnp.int32,(bq,bq),1)
    diag=(tcol==rows)|((tcol<rows)&(tcol<valid_end-start))
    def set_q(shift_lanes):
        x=jnp.concatenate([q[:,:hi],q[:,hi:]+shift_lanes],axis=1)
        for h in range(nh): q_s[h]=x*mask_ref[h:h+1,:]
    self_score=dot(q*own,fold_ref[...],NN)
    shift=self_score.astype(BF).astype(F32)
    sh_s[...]=shift
    set_q(parts(-shift,cols,hi))
    size=jnp.sqrt(dot(q*q,fold_ref[...],NN)*kn_s[:1,:])*1.02
    bounded=jnp.max(size-shift)<=SHIFT_LIMIT
    @pl.when(jnp.logical_not(bounded))
    def _():
        lane=lax.broadcasted_iota(jnp.int32,(bq,LANES),1)+hi-cols
        new=jnp.zeros((bq,LANES),F32)
        for h in range(nh):
            qh=q*mask_ref[h:h+1,:]
            m0=jnp.max(jnp.where(diag,dot(qh,k_s[pl.ds(at,bq),:],NT),-1e30),axis=1,keepdims=True)
            def look(j,m):
                b=row_start+j*bq
                s=dot(qh,k_s[pl.ds(place(sc_ref,b,shard),bq),:],NT)
                s=jnp.where(tcol<valid_end-b,s,-1e30)
                return jnp.maximum(m,jnp.max(s,axis=1,keepdims=True))
            m=lax.fori_loop(0,some,look,m0)
            new=jnp.where((lane>=4*h)&(lane<4*h+4),m,new)
        sh_s[...]=new
        set_q(parts(-new,cols,hi))
    def step(b,masking,first):
        bt=place(sc_ref,b,shard)
        k=k_s[pl.ds(bt,bq),:]
        ps=[]
        for h in range(nh):
            ps.append(dot(q_s[h],k,NT))
        if masking is not None: ps=[jnp.where(masking,s,-1e30) for s in ps]
        ps=[jnp.exp(s).astype(BF) for s in ps]
        new=dot(jnp.concatenate(ps,axis=1),v_s[:,pl.ds(bt,bq),:].reshape(nh*bq,W),NN)
        if first: a_s[...]=new
        else: a_s[...]+=new
    step(start,diag,True)
    def whole(j,c):
        step(row_start+j*bq,None,False); return c
    def partly(j,c):
        b=row_start+j*bq
        step(b,tcol<valid_end-b,False); return c
    def two(j,c):
        b=row_start+2*j*bq
        bts=[place(sc_ref,b,shard),place(sc_ref,b+bq,shard)]
        ps=[dot(q_s[h],k_s[pl.ds(bt,bq),:],NT) for bt in bts for h in range(nh)]
        ps=[jnp.exp(s).astype(BF) for s in ps]
        vs=jnp.concatenate([v_s[:,pl.ds(bt,bq),:].reshape(nh*bq,W) for bt in bts],axis=0)
        a_s[...]+=dot(jnp.concatenate(ps,axis=1),vs,NN)
        return c
    lax.fori_loop(0,full//2,two,0)
    lax.fori_loop(full//2*2,full,whole,0)
    lax.fori_loop(full,some,partly,0)
    total=a_s[:,hi:]
    lane=lax.broadcasted_iota(jnp.int32,(bq,LANES),1)+hi-cols
    spare=(lane>=0)&(lane<4*nh)
    total=jnp.where(spare,total,1.0)
    out=(a_s[:,:cols]*dot(parts(1.0/total,cols,hi),spread_ref[...],NN)[:,:cols]).astype(BF)
    for s in range(n):
        @pl.when(at//shard==s)
        def _(): o_refs[s][pl.ds(pl.multiple_of(at%shard,bq),bq),:]=out
    lse=jnp.where(spare,sh_s[...]+jnp.log(total),0.0)
    qx_ref[...]=jnp.concatenate([q[:,:hi],q[:,hi:]+parts(-lse,cols,hi)],axis=1)

def const(a): return pl.BlockSpec(a.shape,lambda i,sc:(0,)*a.ndim)

def attn_fwd(scal, packed, shard, nh=3, bq=512):
    T=packed.shape[0]; W=packed.shape[1]//3
    tabs=tables(nh,W)
    def where(i,sc):
        per=shard//bq
        return (jnp.bitwise_xor(i//per,sc[0])*per+i%per,0)
    return pl.pallas_call(
        functools.partial(fwd_kernel,nh,bq,shard),
        grid_spec=pltpu.PrefetchScalarGridSpec(num_scalar_prefetch=1,grid=(T//bq,),
            in_specs=[once(packed)]+[once(a) for a in tabs],
            out_specs=[pl.BlockSpec((shard,nh*HD),lambda i,sc:(0,0))]*(T//shard)+[pl.BlockSpec((bq,W),where)],
            scratch_shapes=[pltpu.VMEM((nh,bq,W),BF),pltpu.VMEM((T,W),BF),pltpu.VMEM((nh,T,W),BF),
                pltpu.VMEM((8,LANES),F32),pltpu.VMEM((bq,LANES),F32),pltpu.VMEM((bq,W),F32)]),
        out_shape=[jax.ShapeDtypeStruct((shard,nh*HD),BF)]*(T//shard)+[jax.ShapeDtypeStruct((T,W),BF)],
        compiler_params=pltpu.CompilerParams(vmem_limit_bytes=56*2**20),
        name="attention_forward",
    )(scal,packed,*tabs)

def bwd_kernel(nh,heads,n,bk,shard,sc_ref,qx_ref,p_ref,*refs):
    o_refs=refs[:n]; g_refs=refs[n:2*n]; mask_ref,fold_ref=refs[2*n:2*n+2]
    old_ref=refs[2*n+2] if len(refs)>2*n+8 else None
    out_ref,q_s,d_s,dq_s,dk_s,dv_s=refs[-6:]; m=len(heads)
    T=p_ref.shape[0]; W=p_ref.shape[1]//3; hi=W-LANES; cols=nh*HD
    j=pl.program_id(0)
    @pl.when(j==0)
    def _():
        for c in range(0,T,512):
            qx=qx_ref[c:c+512,:]
            g=g_refs[c//shard][c%shard:c%shard+512,:]
            og=o_refs[c//shard][c%shard:c%shard+512,:].astype(F32)*g.astype(F32)
            og1=og.astype(BF); og2=(og-og1.astype(F32)).astype(BF)
            delta=dot(og1,fold_ref[:cols,:],NN)+dot(og2,fold_ref[:cols,:],NN)
            gx=jnp.concatenate([g,jnp.zeros((512,W-cols),BF)],axis=1)
            gx=jnp.concatenate([gx[:,:hi],gx[:,hi:]+parts(-delta,cols,hi)],axis=1)
            for i,h in enumerate(heads):
                q_s[i,c:c+512,:]=qx*mask_ref[h:h+1,:]
                d_s[i,c:c+512,:]=gx*mask_ref[h:h+1,:]
            dq_s[:,c:c+512]=jnp.zeros((m*HD,512),F32)
    start=j*bk
    row_start,valid_end,row_end=row_info(sc_ref,start)
    at=place(sc_ref,start,shard)
    k0=p_ref[pl.ds(at,bk),W:2*W]
    k=k0+mask_ref[nh:nh+1,:]; v=p_ref[pl.ds(at,bk),2*W:]+mask_ref[nh:nh+1,:]
    kt=jnp.transpose(k0)
    def step(i,kind):
        b=start+i*bk
        bt=place(sc_ref,b,shard)
        if kind!=0:
            krow=lax.broadcasted_iota(jnp.int32,(bk,bk),0); qcol=lax.broadcasted_iota(jnp.int32,(bk,bk),1)
            ok=krow<valid_end-start
            if kind==2: ok=(krow==qcol)|((krow<qcol)&ok)
        ss=[dot(k,q_s[i,pl.ds(bt,bk),:],NT) for i in range(m)]
        dps=[dot(v,d_s[i,pl.ds(bt,bk),:],NT) for i in range(m)]
        ps=[];dss=[]
        for s,dp in zip(ss,dps):
            if kind!=0: s=jnp.where(ok,s,-1e30)
            p=jnp.exp(s)
            ps.append(p.astype(BF)); dss.append((p*dp).astype(BF))
        dv=dot(jnp.concatenate(ps,axis=1),d_s[:,pl.ds(bt,bk),:].reshape(m*bk,W),NN)
        dk=dot(jnp.concatenate(dss,axis=1),q_s[:,pl.ds(bt,bk),:].reshape(m*bk,W),NN)
        for i,h in enumerate(heads): dq_s[i*HD:(i+1)*HD,pl.ds(bt,bk)]+=dot(kt[h*HD:(h+1)*HD],dss[i],NN)
        if kind==2: dv_s[...]=dv; dk_s[...]=dk
        else: dv_s[...]+=dv; dk_s[...]+=dk
    after=(row_end-start)//bk
    n_off=jnp.where(valid_end>start,after,1)
    step(0,2)
    whole=valid_end>=start+bk
    lax.fori_loop(1,jnp.where(whole,after,1),lambda i,c:(step(i,0),c)[1],0)
    lax.fori_loop(1,jnp.where(whole,1,n_off),lambda i,c:(step(i,1),c)[1],0)
    keep=(lax.broadcasted_iota(jnp.int32,(bk,W),1)<cols)
    def put(rows,at_lane,x):
        x=x.astype(BF)
        if old_ref is not None: x=x+old_ref[rows,at_lane:at_lane+W]
        out_ref[rows,at_lane:at_lane+W]=x
    put(pl.ds(at,bk),W,jnp.where(keep,dk_s[...],0.0))
    put(pl.ds(at,bk),2*W,jnp.where(keep,dv_s[...],0.0))
    @pl.when(j==pl.num_programs(0)-1)
    def _():
        for c in range(0,T,512):
            first=heads[0]*HD; rest=W-first-m*HD
            x=dq_s[:,c:c+512]
            if first: x=jnp.concatenate([jnp.zeros((first,512),F32),x],axis=0)
            if rest: x=jnp.concatenate([x,jnp.zeros((rest,512),F32)],axis=0)
            put(slice(c,c+512),0,jnp.transpose(x))

def once(a): return pl.BlockSpec(a.shape,lambda i,sc:(0,)*a.ndim,pipeline_mode=pl.Buffered(1))

def attn_bwd(scal,qx,packed,attn,grads,shard,nh,heads,old=None,bk=512):
    T=packed.shape[0]; W=packed.shape[1]//3; m=len(heads)
    masks,fold,spread=tables(nh,W)
    more=[] if old is None else [old]
    args=[qx,packed,*attn,*grads,masks,fold]+more
    return pl.pallas_call(
        functools.partial(bwd_kernel,nh,heads,len(grads),bk,shard),
        grid_spec=pltpu.PrefetchScalarGridSpec(num_scalar_prefetch=1,grid=(T//bk,),
            in_specs=[once(x) for x in args],
            out_specs=const(packed),
            scratch_shapes=[pltpu.VMEM((m,T,W),BF),pltpu.VMEM((m,T,W),BF),pltpu.VMEM((m*HD,T),F32),
                pltpu.VMEM((bk,W),F32),pltpu.VMEM((bk,W),F32)]),
        out_shape=jax.ShapeDtypeStruct(packed.shape,BF),
        compiler_params=pltpu.CompilerParams(vmem_limit_bytes=60*2**20),
        name="attention_backward",
    )(scal,*args)


EPSILON = 1e-05
TN=(((0,),(0,)),((),()))
VMEM_LIMIT=60*2**20


def widen(ref, buf):
    buf[:,:ref.shape[1]]=ref[...].astype(F32)
    lane=lax.broadcasted_iota(jnp.int32,buf.shape,1)
    return jnp.where(lane<ref.shape[1],buf[...],0.0)

def closed(x):
    lane=lax.broadcasted_iota(jnp.int32,x.shape,1)
    return jnp.where(lane<x.shape[1]-1,x,-jnp.sum(x,axis=1,keepdims=True))

def last_off(x):
    return x-x[:,x.shape[1]-1:]

def centred(x):
    return x-jnp.mean(x,axis=1,keepdims=True)

def inverse(z):
    return lax.rsqrt(jnp.mean(z*z,axis=1,keepdims=True)+EPSILON)

def norm_pull(grad,hat,inv,gain):
    dh=grad*gain
    return last_off((dh-hat*jnp.mean(dh*hat,axis=1,keepdims=True))*inv)

def first_norm_kernel(x_ref,gain_ref,n_ref,buf):
    z=closed(widen(x_ref,buf))
    n_ref[...]=(z*inverse(z)*gain_ref[...]).astype(BF)

def first_norm(stream,gain):
    T,C=stream.shape; R=min(T,256)
    return pl.pallas_call(first_norm_kernel,grid=(T//R,),
        in_specs=[pl.BlockSpec((R,C),lambda i:(i,0)),pl.BlockSpec((1,C+1),lambda i:(0,0))],
        out_specs=pl.BlockSpec((R,C+1),lambda i:(i,0)),
        out_shape=jax.ShapeDtypeStruct((T,C+1),BF),
        scratch_shapes=[pltpu.VMEM((R,C+1),F32)],name="first_norm")(stream,gain)

def project_kernel(sc_ref,x_ref,w_ref,*refs):
    refs[-1][...]=dot(x_ref[...],w_ref[...],NN).astype(BF)

def project(scal,x,w,count,at,old=None):
    T,D=x.shape; N=w.shape[1]; R=T//2
    more=[] if old is None else [old]
    return pl.pallas_call(project_kernel,
        grid_spec=pltpu.PrefetchScalarGridSpec(num_scalar_prefetch=1,grid=(T//R,),
            in_specs=[pl.BlockSpec((R,D),lambda i,sc:(i,0)),const(w)]+[pl.BlockSpec(memory_space=pl.ANY)]*len(more),
            out_specs=pl.BlockSpec((R,N),lambda i,sc:(at*(T//R)+i,0))),
        out_shape=jax.ShapeDtypeStruct((count*T,N),BF),
        input_output_aliases={3:0} if more else {},
        compiler_params=pltpu.CompilerParams(vmem_limit_bytes=VMEM_LIMIT),
        name="project")(scal,x,w,*more)

def last_norm_kernel(x_ref,mid_ref,a_ref,b_ref,c_ref,gain_ref,out_ref,buf):
    z=closed(widen(x_ref,buf))
    inv=inverse(z)
    grad=(a_ref[...].astype(F32)+b_ref[...].astype(F32))+c_ref[...].astype(F32)
    out=mid_ref[...]+norm_pull(grad,z*inv,inv,gain_ref[...])
    out_ref[...]=out[:,:out_ref.shape[1]]

def last_norm(stream,middle,terms,gain):
    T,C=stream.shape; R=min(T,256)
    row=lambda w: pl.BlockSpec((R,w),lambda i:(i,0))
    return pl.pallas_call(last_norm_kernel,grid=(T//R,),
        in_specs=[row(C)]+[row(C+1)]*4+[pl.BlockSpec((1,C+1),lambda i:(0,0))],
        out_specs=row(C),out_shape=jax.ShapeDtypeStruct((T,C),F32),
        scratch_shapes=[pltpu.VMEM((R,C+1),F32)],name="last_norm")(stream,middle,*terms,gain)

def piece_order(n):
    return [i for i in range(n) if i&1]+[i for i in range(n) if not i&1]

def middle_kernel(n,R,sc_ref,x_ref,c_ref,gain_ref,*refs):
    attn=refs[:n]; outw=refs[n:2*n]; weights=refs[2*n:3*n]; gh=refs[3*n:4*n]
    res_ref,mid_ref,send_ref,keep_ref,go_ref,sum_ref,buf,z_s,n_s,g_s,bm_s,gn_s,w_s,wu_s,wd_s,sem=refs[4*n:]
    T,D=z_s.shape; H=attn[0].shape[1]; FD=w_s.shape[1]//2; tiles=T//R
    k=pl.program_id(0); order=piece_order(n)
    lane=lax.broadcasted_iota(jnp.int32,(R,D),1)
    def fetch(s,slot): return pltpu.make_async_copy(weights[s].at[H:,:],w_s.at[slot],sem.at[slot])
    def rows(r): return pl.ds(pl.multiple_of(r*R,R),R)
    def valid_rows(r):
        start=sc_ref[16]+r*R
        return lax.broadcasted_iota(jnp.int32,(R,D),0)<row_info(sc_ref,start)[1]-start
    def grad_out(r):
        buf[:,:D-1]=c_ref[rows(r),:].astype(F32)
        return jnp.where((lane<D-1)&valid_rows(r),buf[...],0.0)
    def squares(x,r):
        x=jnp.where(valid_rows(r),x,0.0)
        return jnp.sum((x*x).reshape(R//8,8,D),axis=0)
    @pl.when(k==0)
    def _():
        fetch(order[0],0).start()
        sum_ref[...]=jnp.zeros_like(sum_ref)
        def first(r,carry):
            at=rows(r)
            buf[:,:D-1]=x_ref[at,:].astype(F32)
            z1=closed(jnp.where(lane<D-1,buf[...],0.0))
            ba=sum(dot(attn[s][at,:],outw[s][...],NN) for s in range(n))
            z2=z1+centred(ba)
            z_s[at,:]=z2
            n_s[at,:]=(z2*inverse(z2)*gain_ref[...]).astype(BF)
            g_s[at,:]=centred(grad_out(r)).astype(BF)
            bm_s[at,:]=jnp.zeros((R,D),F32); gn_s[at,:]=jnp.zeros((R,D),F32)
            sum_ref[16:24,:]+=squares(ba,r)
            return carry
        lax.fori_loop(0,tiles,first,0)
    slot=k%2
    for s in range(n):
        @pl.when(k==s)
        def _():
            fetch(order[s],s%2).wait()
            if s+1<n: fetch(order[s+1],(s+1)%2).start()
    def piece(r,carry):
        at=rows(r)
        nr=n_s[at,:]; gr=g_s[at,:]
        up=w_s[slot,:FD,:]; down=w_s[slot,FD:,:]
        x=dot(nr,up,NN)
        sq=x*x
        th=jnp.tanh(x*(0.7978845608028654+0.035677408136300125*sq))
        half=0.5+0.5*th
        hid=(x*half).astype(BF)
        slope=half+0.5*x*(1.0-th*th)*(0.7978845608028654+0.10703222440890037*sq)
        gp=(dot(gr,down,NT)*slope).astype(BF)
        bm_s[at,:]+=dot(hid,down,NN); gn_s[at,:]+=dot(gp,up,NT)
        wu_s[...]+=dot(nr,gp,TN); wd_s[...]+=dot(hid,gr,TN)
        return carry
    wu_s[...]=jnp.zeros_like(wu_s); wd_s[...]=jnp.zeros_like(wd_s)
    lax.fori_loop(0,tiles,piece,0)
    def put(ref):
        ref[0,:FD,:]=wu_s[...].astype(BF); ref[0,FD:,:]=wd_s[...].astype(BF)
    pl.when(k<n//2)(functools.partial(put,send_ref))
    pl.when(k>=n//2)(functools.partial(put,keep_ref))
    @pl.when(k==n-1)
    def _():
        def final(r,carry):
            at=rows(r)
            z2=z_s[at,:]; inv=inverse(z2); hat=z2*inv; gn=gn_s[at,:]; bm=bm_s[at,:]
            out=z2+centred(bm)
            res_ref[at,:]=out[:,:D-1].astype(BF)
            mid=grad_out(r)+norm_pull(gn,hat,inv,gain_ref[...])
            mid_ref[at,:]=mid
            ga=centred(mid).astype(BF)
            g_s[at,:]=ga
            for s in range(n): gh[s][at,:]=dot(ga,outw[s][...],NT).astype(BF)
            sum_ref[0:8,:]+=jnp.sum((gn*hat).reshape(R//8,8,D),axis=0)
            sum_ref[8:16,:]+=squares(out,r); sum_ref[24:32,:]+=squares(bm,r)
            return carry
        lax.fori_loop(0,tiles,final,0)
        for s in range(n): go_ref[s]=dot(attn[order[s]][...],g_s[...],TN).astype(BF)

def middle_part(scal,stream,cotangent,gain,attn,weights,R=256):
    n=len(attn); T,H=attn[0].shape; D=stream.shape[1]+1; FD=(weights[0].shape[0]-H)//2; R=min(R,T)
    once=lambda a: pl.BlockSpec(a.shape,lambda i,sc:(0,)*a.ndim,pipeline_mode=pl.Buffered(1))
    whole=lambda *s: pl.BlockSpec(s,lambda i,sc:(0,)*len(s))
    top=pl.BlockSpec((H,D),lambda i,sc:(0,0),pipeline_mode=pl.Buffered(1))
    return pl.pallas_call(
        functools.partial(middle_kernel,n,R),
        grid_spec=pltpu.PrefetchScalarGridSpec(num_scalar_prefetch=1,grid=(n,),
            in_specs=[once(stream),once(cotangent),once(gain)]+[once(a) for a in attn]+[top]*n+[pl.BlockSpec(memory_space=pl.ANY)]*n,
            out_specs=[whole(T,H)]*n+[whole(T,D-1),whole(T,D),pl.BlockSpec((1,2*FD,D),lambda i,sc:(jnp.minimum(i,n//2-1),0,0)),
                pl.BlockSpec((1,2*FD,D),lambda i,sc:(jnp.maximum(i-n//2,0),0,0)),whole(n,H,D),whole(32,D)],
            scratch_shapes=[pltpu.VMEM((R,D),F32),pltpu.VMEM((T,D),F32),pltpu.VMEM((T,D),BF),pltpu.VMEM((T,D),BF),pltpu.VMEM((T,D),F32),pltpu.VMEM((T,D),F32),
                pltpu.VMEM((2,2*FD,D),BF),pltpu.VMEM((D,FD),F32),pltpu.VMEM((FD,D),F32),pltpu.SemaphoreType.DMA((2,))]),
        out_shape=[jax.ShapeDtypeStruct((T,H),BF)]*n+[jax.ShapeDtypeStruct((T,D-1),BF),jax.ShapeDtypeStruct((T,D),F32),
            jax.ShapeDtypeStruct((n//2,2*FD,D),BF),jax.ShapeDtypeStruct((n//2,2*FD,D),BF),jax.ShapeDtypeStruct((n,H,D),BF),jax.ShapeDtypeStruct((32,D),F32)],
        compiler_params=pltpu.CompilerParams(vmem_limit_bytes=VMEM_LIMIT),
        name="middle",
    )(scal,stream,cotangent,gain,*attn,*weights,*weights)


def swap(x,axis,step):
    size=lax.axis_size(axis)
    return lax.ppermute(x,axis,[(i,i^step) for i in range(size)])

def after(x,*others):
    return lax.optimization_barrier((x,)+others)[0]

def choose(options,index):
    out=options[0]
    for i in range(1,len(options)): out=jnp.where(index==i,options[i],out)
    return out

def bit_groups(size):
    bits=[1<<b for b in range(size.bit_length()-1)]
    groups=[bits[:1]]; rest=bits[1:]
    while rest: groups.append(rest[:2]); rest=rest[2:]
    return [g for g in groups if g]

def scatter_stage(cur,axis,bits):
    m=1<<len(bits); low=bits[0]; mine=(lax.axis_index(axis)//low)%m
    rows=cur.shape[0]//m
    cut=[cur[i*rows:(i+1)*rows] for i in range(m)]
    total=choose(cut,mine)
    for d in range(1,m):
        total=total+swap(choose([cut[i^d] for i in range(m)],mine).astype(BF),axis,d*low).astype(F32)
    return total

def gather_stage(cur,axis,bits):
    m=1<<len(bits); low=bits[0]; mine=(lax.axis_index(axis)//low)%m
    got=[cur]+[swap(cur,axis,d*low) for d in range(1,m)]
    return jnp.concatenate([choose([got[i^p] for i in range(m)],mine) for p in range(m)],axis=0)

def butterfly(x,axis):
    step=1
    while step<lax.axis_size(axis):
        x=x+swap(x,axis,step); step*=2
    return x

def shards(stream,cotangent,bucket,row_counts,lengths,w_qkv,w_out,w_up,w_down,gain_one,gain_two):
    T=stream.shape[0]; D=stream.shape[1]+1; C=w_qkv.shape[2]; nh=C//HD
    n=lax.axis_size("tensor"); t=lax.axis_index("tensor")
    wide=-(-(C+4*nh)//LANES)*LANES
    span=BASE*jnp.where(bucket[0]==0,1,jnp.where(bucket[0]==1,2,4)).astype(jnp.int32)
    zero=jnp.zeros((),jnp.int32)
    scal=jnp.stack([t.astype(jnp.int32),span,row_counts[0]]+[lengths[0,r] for r in range(lengths.shape[1])]+[zero]*(13-lengths.shape[1])+[(t*T).astype(jnp.int32)])
    g1=gain_one.reshape(1,D); g2=gain_two.reshape(1,D)
    lift=np.ones((1,3,1),np.float32); lift[0,0]=HD**-0.5
    w_pad=jnp.pad(w_qkv*jnp.asarray(lift,BF),((0,0),(0,0),(0,wide-C))).reshape(D,3*wide)

    normed=first_norm(stream,g1)
    far=swap(normed,"tensor",2); near=swap(normed,"tensor",1)
    own_w=jnp.concatenate([w_out,w_up,w_down],axis=0)
    near_w=swap(own_w,"tensor",1)
    packed=project(scal,normed,w_pad,n,0)
    near,near_w=lax.optimization_barrier((near,near_w))
    packed=project(scal,near,w_pad,n,1,packed)
    far,packed=lax.optimization_barrier((far,packed))
    far_w=swap(after(own_w,far),"tensor",2)
    corner=swap(far,"tensor",1)
    packed=project(scal,far,w_pad,n,2,packed)
    packed=project(scal,corner,w_pad,n,3,packed)
    *heads_out,qx=attn_fwd(scal,packed,T,nh)
    attn=[heads_out[0]]+[swap(heads_out[d],"tensor",d) for d in range(1,n)]
    weights=[own_w,near_w,far_w,swap(after(far_w,attn[1]),"tensor",1)]
    *grad_heads,result,mid,w_send,w_keep,go,sums=middle_part(scal,stream,cotangent,g2,attn,weights)
    heads=[grad_heads[0]]+[swap(grad_heads[d],"tensor",d) for d in range(1,n)]
    w_got=swap(w_send,"tensor",1); o_got=swap(go[:n//2],"tensor",1)
    w_got,o_got,*heads=lax.optimization_barrier((w_got,o_got,*heads))
    R=C+w_keep.shape[1]; q=lax.axis_size("dp"); r=R//q
    flat=lambda x: x.reshape(q,-1,D)
    w_half=(w_keep.astype(F32)+w_got.astype(F32)).astype(BF); o_half=(go[n//2:].astype(F32)+o_got.astype(F32)).astype(BF)
    w_half=jnp.concatenate([flat(x) for i in range(2) for x in (o_half[i],w_half[i,:D],w_half[i,D:])],axis=1).reshape(2*R,D)
    w_part=lax.psum_scatter(w_half,"dp",scatter_dimension=0,tiled=True)

    grad_packed=attn_bwd(scal,qx,packed,heads_out,heads,T,nh,list(range(nh)))
    gathered=jnp.concatenate([normed,near,far,corner],axis=0)
    w_part,grad_packed=lax.optimization_barrier((w_part,grad_packed))
    w_other=swap(w_part[r:],"tensor",2)
    gq=dot(gathered,grad_packed,TN)
    gq=(gq.reshape(D,3,wide)[:,:,:C]*lift).reshape(D,3*C)
    w_own=(w_part[:r].astype(F32)+w_other.astype(F32)).astype(BF)
    gq,w_own,grad_packed=lax.optimization_barrier((gq,w_own,grad_packed))
    w_sum=lax.all_gather(w_own,"dp",axis=0).astype(F32)
    gain_part=jnp.sum(gq.reshape(D,3,C)*w_qkv.astype(F32),axis=(1,2))/gain_one
    def back(i): return dot(grad_packed[i*T:(i+1)*T],w_pad,NT).astype(BF)
    groups=bit_groups(q)
    stage=scatter_stage(gq,"dp",groups[0])
    back_1,back_3=back(1),back(3)
    stage,back_1,back_3,grad_packed=lax.optimization_barrier((stage,back_1,back_3,grad_packed))
    near_0=swap(back_1,"tensor",1); near_2=swap(back_3,"tensor",1)
    back_2=back(2)
    two=(back_2.astype(F32)+near_2.astype(F32)).astype(BF)
    stage,two,grad_packed=lax.optimization_barrier((stage,two,grad_packed))
    far_b=swap(two,"tensor",2)
    for bits in groups[1:]: stage=scatter_stage(stage,"dp",bits)
    stage=stage.astype(BF)
    for bits in groups[:0:-1]: stage=gather_stage(stage,"dp",bits)
    back_0=back(0); spread=stage
    grad_stream=last_norm(stream,mid,[back_0,near_0,far_b],g1)
    stage,grad_stream=lax.optimization_barrier((stage,grad_stream))
    gq=gather_stage(stage,"dp",groups[0]).astype(F32).reshape(D,3,C)
    cut=[0]
    for part in (C,D,w_keep.shape[1]-D): cut.append(cut[-1]+part//q)
    g_out,g_up,g_down=[w_sum[:,i:j].reshape(-1,D) for i,j in zip(cut[:-1],cut[1:])]
    group_tokens=jnp.sum(jnp.where(jnp.arange(lengths.shape[1])<row_counts[0],lengths[0],0)).astype(F32)/n
    s=sums.reshape(4,8,D)
    small=jnp.concatenate([gain_part,jnp.sum(s[0],axis=0),jnp.sum(s[1:],axis=(1,2)),group_tokens[None]])
    small=jnp.pad(small,(0,-small.shape[0]%LANES)).reshape(-1,LANES)
    small=after(small,spread)
    small=butterfly(butterfly(small,"tensor"),"dp").reshape(-1)
    root=jnp.sqrt(small[2*D:2*D+3]/(D*small[2*D+3]))
    return (result,grad_stream,gq,g_out,g_up,g_down,small[:D],small[D:2*D],root)


def solution(mesh):
    rows=P(("dp","tensor"),None)
    return jax.shard_map(shards,mesh=mesh,
        in_specs=(rows,rows,P("dp"),P("dp"),P("dp",None),P(None,None,"tensor"),P("tensor",None),P(None,"tensor"),P("tensor",None),P(),P()),
        out_specs=(rows,rows,P(None,None,"tensor"),P("tensor",None),P(None,"tensor"),P("tensor",None),P(),P(),P()),
        check_vma=False)
```

```python
import functools
import jax, jax.numpy as jnp, numpy as np
from jax import lax
from jax.experimental import pallas as pl
from jax.experimental.pallas import tpu as pltpu
from jax.sharding import PartitionSpec as P
HD=64; BASE=1024
LANES=128
SHIFT_LIMIT=70.0
F32=jnp.float32; BF=jnp.bfloat16
NT=(((1,),(1,)),((),()))
NN=(((1,),(0,)),((),()))
def dot(a,b,dims): return lax.dot_general(a,b,dims,preferred_element_type=F32)

def tables(nh, wide):
    cols=nh*HD; lane=np.arange(wide)
    head=np.where(lane<cols,lane//HD,np.where(lane<cols+4*nh,(lane-cols)//4,-1))
    spare=(lane>=cols)&(lane<cols+4*nh)
    masks=np.zeros((8,wide),np.float32)
    for h in range(nh): masks[h]=(head==h)
    masks[nh]=spare
    for h in range(nh): masks[nh+1+h]=spare&(head==h)
    fold=np.zeros((wide,LANES),np.float32)
    hi=wide-LANES
    same=(head[:,None]==head[None,hi:])&(head[:,None]>=0)
    fold[:]=same&(lane<cols)[:,None]&spare[None,hi:]
    spread=np.zeros((LANES,wide),np.float32)
    spread[:]=(same&(lane<cols)[:,None]&spare[None,hi:]).T
    return jnp.asarray(masks,BF),jnp.asarray(fold,BF),jnp.asarray(spread,BF)

def row_info(sc_ref, start):
    span=sc_ref[1]
    row=start//span
    length=sc_ref[3]
    for r in range(1,4):
        length=jnp.where(row==r, sc_ref[3+r], length)
    length=jnp.where(row<sc_ref[2], length, 0)
    return row*span, row*span+length, row*span+span

def place(sc_ref, start, shard):
    return pl.multiple_of((jnp.bitwise_xor(start//shard, sc_ref[0]))*shard + start%shard, 256)

def parts(x, cols, hi):
    lane=lax.broadcasted_iota(jnp.int32,x.shape,1)+hi-cols
    which=jnp.where(lane<0,3,lane%4)
    a=x.astype(BF).astype(F32); r=x-a; b=r.astype(BF).astype(F32); c=r-b
    return jnp.where(which==0,a,jnp.where(which==1,b,jnp.where(which==2,c,0.0))).astype(BF)

def fwd_kernel(nh, bq, shard, sc_ref, p_ref, mask_ref, fold_ref, spread_ref, *refs):
    n=p_ref.shape[0]//shard; o_refs=refs[:n]; qx_ref, q_s, k_s, v_s, kn_s, sh_s, a_s=refs[n:]
    T=p_ref.shape[0]; W=p_ref.shape[1]//3; hi=W-LANES; cols=nh*HD
    i=pl.program_id(0)
    @pl.when(i==0)
    def _():
        kn=jnp.zeros((8,LANES),F32)
        for c in range(0,T,512):
            k=p_ref[c:c+512,W:2*W]; v=p_ref[c:c+512,2*W:]
            k_s[c:c+512,:]=k+mask_ref[nh:nh+1,:]
            kn=jnp.maximum(kn,jnp.max(dot(k*k,fold_ref[...],NN).reshape(64,8,LANES),axis=0))
            for h in range(nh):
                v_s[h,c:c+512,:]=v*mask_ref[h:h+1,:]+mask_ref[nh+1+h:nh+2+h,:]
        kn_s[...]=jnp.broadcast_to(jnp.max(kn,axis=0,keepdims=True),(8,LANES))
    start=i*bq
    row_start,valid_end,_=row_info(sc_ref,start)
    at=place(sc_ref,start,shard)
    q=p_ref[pl.ds(at,bq),:W]; own=p_ref[pl.ds(at,bq),W:2*W]
    before=(start-row_start)//bq
    full=jnp.minimum(before,(valid_end-row_start)//bq)
    some=jnp.minimum(before,(valid_end-row_start+bq-1)//bq)
    rows=lax.broadcasted_iota(jnp.int32,(bq,bq),0); tcol=lax.broadcasted_iota(jnp.int32,(bq,bq),1)
    diag=(tcol==rows)|((tcol<rows)&(tcol<valid_end-start))
    def set_q(shift_lanes):
        x=jnp.concatenate([q[:,:hi],q[:,hi:]+shift_lanes],axis=1)
        for h in range(nh): q_s[h]=x*mask_ref[h:h+1,:]
    self_score=dot(q*own,fold_ref[...],NN)
    shift=self_score.astype(BF).astype(F32)
    sh_s[...]=shift
    set_q(parts(-shift,cols,hi))
    size=jnp.sqrt(dot(q*q,fold_ref[...],NN)*kn_s[:1,:])*1.02
    bounded=jnp.max(size-shift)<=SHIFT_LIMIT
    @pl.when(jnp.logical_not(bounded))
    def _():
        lane=lax.broadcasted_iota(jnp.int32,(bq,LANES),1)+hi-cols
        new=jnp.zeros((bq,LANES),F32)
        for h in range(nh):
            qh=q*mask_ref[h:h+1,:]
            m0=jnp.max(jnp.where(diag,dot(qh,k_s[pl.ds(at,bq),:],NT),-1e30),axis=1,keepdims=True)
            def look(j,m):
                b=row_start+j*bq
                s=dot(qh,k_s[pl.ds(place(sc_ref,b,shard),bq),:],NT)
                s=jnp.where(tcol<valid_end-b,s,-1e30)
                return jnp.maximum(m,jnp.max(s,axis=1,keepdims=True))
            m=lax.fori_loop(0,some,look,m0)
            new=jnp.where((lane>=4*h)&(lane<4*h+4),m,new)
        sh_s[...]=new
        set_q(parts(-new,cols,hi))
    def step(b,masking,first):
        bt=place(sc_ref,b,shard)
        k=k_s[pl.ds(bt,bq),:]
        ps=[]
        for h in range(nh):
            ps.append(dot(q_s[h],k,NT))
        if masking is not None: ps=[jnp.where(masking,s,-1e30) for s in ps]
        ps=[jnp.exp(s).astype(BF) for s in ps]
        new=dot(jnp.concatenate(ps,axis=1),v_s[:,pl.ds(bt,bq),:].reshape(nh*bq,W),NN)
        if first: a_s[...]=new
        else: a_s[...]+=new
    step(start,diag,True)
    def whole(j,c):
        step(row_start+j*bq,None,False); return c
    def partly(j,c):
        b=row_start+j*bq
        step(b,tcol<valid_end-b,False); return c
    def two(j,c):
        b=row_start+2*j*bq
        bts=[place(sc_ref,b,shard),place(sc_ref,b+bq,shard)]
        ps=[dot(q_s[h],k_s[pl.ds(bt,bq),:],NT) for bt in bts for h in range(nh)]
        ps=[jnp.exp(s).astype(BF) for s in ps]
        vs=jnp.concatenate([v_s[:,pl.ds(bt,bq),:].reshape(nh*bq,W) for bt in bts],axis=0)
        a_s[...]+=dot(jnp.concatenate(ps,axis=1),vs,NN)
        return c
    lax.fori_loop(0,full//2,two,0)
    lax.fori_loop(full//2*2,full,whole,0)
    lax.fori_loop(full,some,partly,0)
    total=a_s[:,hi:]
    lane=lax.broadcasted_iota(jnp.int32,(bq,LANES),1)+hi-cols
    spare=(lane>=0)&(lane<4*nh)
    total=jnp.where(spare,total,1.0)
    out=(a_s[:,:cols]*dot(parts(1.0/total,cols,hi),spread_ref[...],NN)[:,:cols]).astype(BF)
    for s in range(n):
        @pl.when(at//shard==s)
        def _(): o_refs[s][pl.ds(pl.multiple_of(at%shard,bq),bq),:]=out
    lse=jnp.where(spare,sh_s[...]+jnp.log(total),0.0)
    qx_ref[...]=jnp.concatenate([q[:,:hi],q[:,hi:]+parts(-lse,cols,hi)],axis=1)

def const(a): return pl.BlockSpec(a.shape,lambda i,sc:(0,)*a.ndim)

def attn_fwd(scal, packed, shard, nh=3, bq=512):
    T=packed.shape[0]; W=packed.shape[1]//3
    tabs=tables(nh,W)
    def where(i,sc):
        per=shard//bq
        return (jnp.bitwise_xor(i//per,sc[0])*per+i%per,0)
    return pl.pallas_call(
        functools.partial(fwd_kernel,nh,bq,shard),
        grid_spec=pltpu.PrefetchScalarGridSpec(num_scalar_prefetch=1,grid=(T//bq,),
            in_specs=[once(packed)]+[once(a) for a in tabs],
            out_specs=[pl.BlockSpec((shard,nh*HD),lambda i,sc:(0,0))]*(T//shard)+[pl.BlockSpec((bq,W),where)],
            scratch_shapes=[pltpu.VMEM((nh,bq,W),BF),pltpu.VMEM((T,W),BF),pltpu.VMEM((nh,T,W),BF),
                pltpu.VMEM((8,LANES),F32),pltpu.VMEM((bq,LANES),F32),pltpu.VMEM((bq,W),F32)]),
        out_shape=[jax.ShapeDtypeStruct((shard,nh*HD),BF)]*(T//shard)+[jax.ShapeDtypeStruct((T,W),BF)],
        compiler_params=pltpu.CompilerParams(vmem_limit_bytes=56*2**20),
        name="attention_forward",
    )(scal,packed,*tabs)

def bwd_kernel(nh,heads,n,bk,shard,sc_ref,qx_ref,p_ref,*refs):
    o_refs=refs[:n]; g_refs=refs[n:2*n]; mask_ref,fold_ref=refs[2*n:2*n+2]
    old_ref=refs[2*n+2] if len(refs)>2*n+8 else None
    out_ref,q_s,d_s,dq_s,dk_s,dv_s=refs[-6:]; m=len(heads)
    T=p_ref.shape[0]; W=p_ref.shape[1]//3; hi=W-LANES; cols=nh*HD
    j=pl.program_id(0)
    @pl.when(j==0)
    def _():
        for c in range(0,T,512):
            qx=qx_ref[c:c+512,:]
            g=g_refs[c//shard][c%shard:c%shard+512,:]
            og=o_refs[c//shard][c%shard:c%shard+512,:].astype(F32)*g.astype(F32)
            og1=og.astype(BF); og2=(og-og1.astype(F32)).astype(BF)
            delta=dot(og1,fold_ref[:cols,:],NN)+dot(og2,fold_ref[:cols,:],NN)
            gx=jnp.concatenate([g,jnp.zeros((512,W-cols),BF)],axis=1)
            gx=jnp.concatenate([gx[:,:hi],gx[:,hi:]+parts(-delta,cols,hi)],axis=1)
            for i,h in enumerate(heads):
                q_s[i,c:c+512,:]=qx*mask_ref[h:h+1,:]
                d_s[i,c:c+512,:]=gx*mask_ref[h:h+1,:]
            dq_s[:,c:c+512]=jnp.zeros((m*HD,512),F32)
    start=j*bk
    row_start,valid_end,row_end=row_info(sc_ref,start)
    at=place(sc_ref,start,shard)
    k0=p_ref[pl.ds(at,bk),W:2*W]
    k=k0+mask_ref[nh:nh+1,:]; v=p_ref[pl.ds(at,bk),2*W:]+mask_ref[nh:nh+1,:]
    kt=jnp.transpose(k0)
    def step(i,kind):
        b=start+i*bk
        bt=place(sc_ref,b,shard)
        if kind!=0:
            krow=lax.broadcasted_iota(jnp.int32,(bk,bk),0); qcol=lax.broadcasted_iota(jnp.int32,(bk,bk),1)
            ok=krow<valid_end-start
            if kind==2: ok=(krow==qcol)|((krow<qcol)&ok)
        ss=[dot(k,q_s[i,pl.ds(bt,bk),:],NT) for i in range(m)]
        dps=[dot(v,d_s[i,pl.ds(bt,bk),:],NT) for i in range(m)]
        ps=[];dss=[]
        for s,dp in zip(ss,dps):
            if kind!=0: s=jnp.where(ok,s,-1e30)
            p=jnp.exp(s)
            ps.append(p.astype(BF)); dss.append((p*dp).astype(BF))
        dv=dot(jnp.concatenate(ps,axis=1),d_s[:,pl.ds(bt,bk),:].reshape(m*bk,W),NN)
        dk=dot(jnp.concatenate(dss,axis=1),q_s[:,pl.ds(bt,bk),:].reshape(m*bk,W),NN)
        for i,h in enumerate(heads): dq_s[i*HD:(i+1)*HD,pl.ds(bt,bk)]+=dot(kt[h*HD:(h+1)*HD],dss[i],NN)
        if kind==2: dv_s[...]=dv; dk_s[...]=dk
        else: dv_s[...]+=dv; dk_s[...]+=dk
    after=(row_end-start)//bk
    n_off=jnp.where(valid_end>start,after,1)
    step(0,2)
    whole=valid_end>=start+bk
    lax.fori_loop(1,jnp.where(whole,after,1),lambda i,c:(step(i,0),c)[1],0)
    lax.fori_loop(1,jnp.where(whole,1,n_off),lambda i,c:(step(i,1),c)[1],0)
    keep=(lax.broadcasted_iota(jnp.int32,(bk,W),1)<cols)
    def put(rows,at_lane,x):
        x=x.astype(BF)
        if old_ref is not None: x=x+old_ref[rows,at_lane:at_lane+W]
        out_ref[rows,at_lane:at_lane+W]=x
    put(pl.ds(at,bk),W,jnp.where(keep,dk_s[...],0.0))
    put(pl.ds(at,bk),2*W,jnp.where(keep,dv_s[...],0.0))
    @pl.when(j==pl.num_programs(0)-1)
    def _():
        for c in range(0,T,512):
            first=heads[0]*HD; rest=W-first-m*HD
            x=dq_s[:,c:c+512]
            if first: x=jnp.concatenate([jnp.zeros((first,512),F32),x],axis=0)
            if rest: x=jnp.concatenate([x,jnp.zeros((rest,512),F32)],axis=0)
            put(slice(c,c+512),0,jnp.transpose(x))

def once(a): return pl.BlockSpec(a.shape,lambda i,sc:(0,)*a.ndim,pipeline_mode=pl.Buffered(1))

def attn_bwd(scal,qx,packed,attn,grads,shard,nh,heads,old=None,bk=512):
    T=packed.shape[0]; W=packed.shape[1]//3; m=len(heads)
    masks,fold,spread=tables(nh,W)
    more=[] if old is None else [old]
    args=[qx,packed,*attn,*grads,masks,fold]+more
    return pl.pallas_call(
        functools.partial(bwd_kernel,nh,heads,len(grads),bk,shard),
        grid_spec=pltpu.PrefetchScalarGridSpec(num_scalar_prefetch=1,grid=(T//bk,),
            in_specs=[once(x) for x in args],
            out_specs=const(packed),
            scratch_shapes=[pltpu.VMEM((m,T,W),BF),pltpu.VMEM((m,T,W),BF),pltpu.VMEM((m*HD,T),F32),
                pltpu.VMEM((bk,W),F32),pltpu.VMEM((bk,W),F32)]),
        out_shape=jax.ShapeDtypeStruct(packed.shape,BF),
        compiler_params=pltpu.CompilerParams(vmem_limit_bytes=60*2**20),
        name="attention_backward",
    )(scal,*args)


EPSILON = 1e-05
TN=(((0,),(0,)),((),()))
VMEM_LIMIT=60*2**20


def widen(ref, buf):
    buf[:,:ref.shape[1]]=ref[...].astype(F32)
    lane=lax.broadcasted_iota(jnp.int32,buf.shape,1)
    return jnp.where(lane<ref.shape[1],buf[...],0.0)

def closed(x):
    lane=lax.broadcasted_iota(jnp.int32,x.shape,1)
    return jnp.where(lane<x.shape[1]-1,x,-jnp.sum(x,axis=1,keepdims=True))

def last_off(x):
    return x-x[:,x.shape[1]-1:]

def centred(x):
    return x-jnp.mean(x,axis=1,keepdims=True)

def inverse(z):
    return lax.rsqrt(jnp.mean(z*z,axis=1,keepdims=True)+EPSILON)

def norm_pull(grad,hat,inv,gain):
    dh=grad*gain
    return last_off((dh-hat*jnp.mean(dh*hat,axis=1,keepdims=True))*inv)

def first_norm_kernel(x_ref,gain_ref,n_ref,buf):
    z=closed(widen(x_ref,buf))
    n_ref[...]=(z*inverse(z)*gain_ref[...]).astype(BF)

def first_norm(stream,gain):
    T,C=stream.shape; R=min(T,256)
    return pl.pallas_call(first_norm_kernel,grid=(T//R,),
        in_specs=[pl.BlockSpec((R,C),lambda i:(i,0)),pl.BlockSpec((1,C+1),lambda i:(0,0))],
        out_specs=pl.BlockSpec((R,C+1),lambda i:(i,0)),
        out_shape=jax.ShapeDtypeStruct((T,C+1),BF),
        scratch_shapes=[pltpu.VMEM((R,C+1),F32)],name="first_norm")(stream,gain)

def project_kernel(sc_ref,x_ref,w_ref,*refs):
    refs[-1][...]=dot(x_ref[...],w_ref[...],NN).astype(BF)

def project(scal,x,w,count,at,old=None):
    T,D=x.shape; N=w.shape[1]; R=T//2
    more=[] if old is None else [old]
    return pl.pallas_call(project_kernel,
        grid_spec=pltpu.PrefetchScalarGridSpec(num_scalar_prefetch=1,grid=(T//R,),
            in_specs=[pl.BlockSpec((R,D),lambda i,sc:(i,0)),const(w)]+[pl.BlockSpec(memory_space=pl.ANY)]*len(more),
            out_specs=pl.BlockSpec((R,N),lambda i,sc:(at*(T//R)+i,0))),
        out_shape=jax.ShapeDtypeStruct((count*T,N),BF),
        input_output_aliases={3:0} if more else {},
        compiler_params=pltpu.CompilerParams(vmem_limit_bytes=VMEM_LIMIT),
        name="project")(scal,x,w,*more)

def last_norm_kernel(x_ref,mid_ref,a_ref,b_ref,c_ref,gain_ref,out_ref,buf):
    z=closed(widen(x_ref,buf))
    inv=inverse(z)
    grad=(a_ref[...].astype(F32)+b_ref[...].astype(F32))+c_ref[...].astype(F32)
    out=mid_ref[...]+norm_pull(grad,z*inv,inv,gain_ref[...])
    out_ref[...]=out[:,:out_ref.shape[1]]

def last_norm(stream,middle,terms,gain):
    T,C=stream.shape; R=min(T,256)
    row=lambda w: pl.BlockSpec((R,w),lambda i:(i,0))
    return pl.pallas_call(last_norm_kernel,grid=(T//R,),
        in_specs=[row(C)]+[row(C+1)]*4+[pl.BlockSpec((1,C+1),lambda i:(0,0))],
        out_specs=row(C),out_shape=jax.ShapeDtypeStruct((T,C),F32),
        scratch_shapes=[pltpu.VMEM((R,C+1),F32)],name="last_norm")(stream,middle,*terms,gain)

def piece_order(n):
    return [i for i in range(n) if i&1]+[i for i in range(n) if not i&1]

def middle_kernel(n,R,sc_ref,x_ref,c_ref,gain_ref,*refs):
    attn=refs[:n]; outw=refs[n:2*n]; weights=refs[2*n:3*n]; gh=refs[3*n:4*n]
    res_ref,mid_ref,send_ref,keep_ref,go_ref,sum_ref,buf,z_s,n_s,g_s,bm_s,gn_s,w_s,wu_s,wd_s,sem=refs[4*n:]
    T,D=z_s.shape; H=attn[0].shape[1]; FD=w_s.shape[1]//2; tiles=T//R
    k=pl.program_id(0); order=piece_order(n)
    lane=lax.broadcasted_iota(jnp.int32,(R,D),1)
    def fetch(s,slot): return pltpu.make_async_copy(weights[s].at[H:,:],w_s.at[slot],sem.at[slot])
    def rows(r): return pl.ds(pl.multiple_of(r*R,R),R)
    def valid_rows(r):
        start=sc_ref[16]+r*R
        return lax.broadcasted_iota(jnp.int32,(R,D),0)<row_info(sc_ref,start)[1]-start
    def grad_out(r):
        buf[:,:D-1]=c_ref[rows(r),:].astype(F32)
        return jnp.where((lane<D-1)&valid_rows(r),buf[...],0.0)
    def squares(x,r):
        x=jnp.where(valid_rows(r),x,0.0)
        return jnp.sum((x*x).reshape(R//8,8,D),axis=0)
    @pl.when(k==0)
    def _():
        fetch(order[0],0).start()
        sum_ref[...]=jnp.zeros_like(sum_ref)
        def first(r,carry):
            at=rows(r)
            buf[:,:D-1]=x_ref[at,:].astype(F32)
            z1=closed(jnp.where(lane<D-1,buf[...],0.0))
            ba=sum(dot(attn[s][at,:],outw[s][...],NN) for s in range(n))
            z2=z1+centred(ba)
            z_s[at,:]=z2
            n_s[at,:]=(z2*inverse(z2)*gain_ref[...]).astype(BF)
            g_s[at,:]=centred(grad_out(r)).astype(BF)
            bm_s[at,:]=jnp.zeros((R,D),F32); gn_s[at,:]=jnp.zeros((R,D),F32)
            sum_ref[16:24,:]+=squares(ba,r)
            return carry
        lax.fori_loop(0,tiles,first,0)
    slot=k%2
    for s in range(n):
        @pl.when(k==s)
        def _():
            fetch(order[s],s%2).wait()
            if s+1<n: fetch(order[s+1],(s+1)%2).start()
    def piece(r,carry):
        at=rows(r)
        nr=n_s[at,:]; gr=g_s[at,:]
        up=w_s[slot,:FD,:]; down=w_s[slot,FD:,:]
        x=dot(nr,up,NN)
        sq=x*x
        th=jnp.tanh(x*(0.7978845608028654+0.035677408136300125*sq))
        half=0.5+0.5*th
        hid=(x*half).astype(BF)
        slope=half+0.5*x*(1.0-th*th)*(0.7978845608028654+0.10703222440890037*sq)
        gp=(dot(gr,down,NT)*slope).astype(BF)
        bm_s[at,:]+=dot(hid,down,NN); gn_s[at,:]+=dot(gp,up,NT)
        wu_s[...]+=dot(nr,gp,TN); wd_s[...]+=dot(hid,gr,TN)
        return carry
    wu_s[...]=jnp.zeros_like(wu_s); wd_s[...]=jnp.zeros_like(wd_s)
    lax.fori_loop(0,tiles,piece,0)
    def put(ref):
        ref[0,:FD,:]=wu_s[...].astype(BF); ref[0,FD:,:]=wd_s[...].astype(BF)
    pl.when(k<n//2)(functools.partial(put,send_ref))
    pl.when(k>=n//2)(functools.partial(put,keep_ref))
    @pl.when(k==n-1)
    def _():
        def final(r,carry):
            at=rows(r)
            z2=z_s[at,:]; inv=inverse(z2); hat=z2*inv; gn=gn_s[at,:]; bm=bm_s[at,:]
            out=z2+centred(bm)
            res_ref[at,:]=out[:,:D-1].astype(BF)
            mid=grad_out(r)+norm_pull(gn,hat,inv,gain_ref[...])
            mid_ref[at,:]=mid
            ga=centred(mid).astype(BF)
            g_s[at,:]=ga
            for s in range(n): gh[s][at,:]=dot(ga,outw[s][...],NT).astype(BF)
            sum_ref[0:8,:]+=jnp.sum((gn*hat).reshape(R//8,8,D),axis=0)
            sum_ref[8:16,:]+=squares(out,r); sum_ref[24:32,:]+=squares(bm,r)
            return carry
        lax.fori_loop(0,tiles,final,0)
        for s in range(n): go_ref[s]=dot(attn[order[s]][...],g_s[...],TN).astype(BF)

def middle_part(scal,stream,cotangent,gain,attn,weights,R=256):
    n=len(attn); T,H=attn[0].shape; D=stream.shape[1]+1; FD=(weights[0].shape[0]-H)//2; R=min(R,T)
    once=lambda a: pl.BlockSpec(a.shape,lambda i,sc:(0,)*a.ndim,pipeline_mode=pl.Buffered(1))
    whole=lambda *s: pl.BlockSpec(s,lambda i,sc:(0,)*len(s))
    top=pl.BlockSpec((H,D),lambda i,sc:(0,0),pipeline_mode=pl.Buffered(1))
    return pl.pallas_call(
        functools.partial(middle_kernel,n,R),
        grid_spec=pltpu.PrefetchScalarGridSpec(num_scalar_prefetch=1,grid=(n,),
            in_specs=[once(stream),once(cotangent),once(gain)]+[once(a) for a in attn]+[top]*n+[pl.BlockSpec(memory_space=pl.ANY)]*n,
            out_specs=[whole(T,H)]*n+[whole(T,D-1),whole(T,D),pl.BlockSpec((1,2*FD,D),lambda i,sc:(jnp.minimum(i,n//2-1),0,0)),
                pl.BlockSpec((1,2*FD,D),lambda i,sc:(jnp.maximum(i-n//2,0),0,0)),whole(n,H,D),whole(32,D)],
            scratch_shapes=[pltpu.VMEM((R,D),F32),pltpu.VMEM((T,D),F32),pltpu.VMEM((T,D),BF),pltpu.VMEM((T,D),BF),pltpu.VMEM((T,D),F32),pltpu.VMEM((T,D),F32),
                pltpu.VMEM((2,2*FD,D),BF),pltpu.VMEM((D,FD),F32),pltpu.VMEM((FD,D),F32),pltpu.SemaphoreType.DMA((2,))]),
        out_shape=[jax.ShapeDtypeStruct((T,H),BF)]*n+[jax.ShapeDtypeStruct((T,D-1),BF),jax.ShapeDtypeStruct((T,D),F32),
            jax.ShapeDtypeStruct((n//2,2*FD,D),BF),jax.ShapeDtypeStruct((n//2,2*FD,D),BF),jax.ShapeDtypeStruct((n,H,D),BF),jax.ShapeDtypeStruct((32,D),F32)],
        compiler_params=pltpu.CompilerParams(vmem_limit_bytes=VMEM_LIMIT),
        name="middle",
    )(scal,stream,cotangent,gain,*attn,*weights,*weights)


def swap(x,axis,step):
    size=lax.axis_size(axis)
    return lax.ppermute(x,axis,[(i,i^step) for i in range(size)])

def after(x,*others):
    return lax.optimization_barrier((x,)+others)[0]

def choose(options,index):
    out=options[0]
    for i in range(1,len(options)): out=jnp.where(index==i,options[i],out)
    return out

def bit_groups(size):
    bits=[1<<b for b in range(size.bit_length()-1)]
    groups=[bits[:1]]; rest=bits[1:]
    while rest: groups.append(rest[:2]); rest=rest[2:]
    return [g for g in groups if g]

def scatter_stage(cur,axis,bits):
    m=1<<len(bits); low=bits[0]; mine=(lax.axis_index(axis)//low)%m
    rows=cur.shape[0]//m
    cut=[cur[i*rows:(i+1)*rows] for i in range(m)]
    total=choose(cut,mine)
    for d in range(1,m):
        total=total+swap(choose([cut[i^d] for i in range(m)],mine).astype(BF),axis,d*low).astype(F32)
    return total

def gather_stage(cur,axis,bits):
    m=1<<len(bits); low=bits[0]; mine=(lax.axis_index(axis)//low)%m
    got=[cur]+[swap(cur,axis,d*low) for d in range(1,m)]
    return jnp.concatenate([choose([got[i^p] for i in range(m)],mine) for p in range(m)],axis=0)

def butterfly(x,axis):
    step=1
    while step<lax.axis_size(axis):
        x=x+swap(x,axis,step); step*=2
    return x

def shards(stream,cotangent,bucket,row_counts,lengths,w_qkv,w_out,w_up,w_down,gain_one,gain_two):
    T=stream.shape[0]; D=stream.shape[1]+1; C=w_qkv.shape[2]; nh=C//HD
    n=lax.axis_size("tensor"); t=lax.axis_index("tensor")
    wide=-(-(C+4*nh)//LANES)*LANES
    span=BASE*jnp.where(bucket[0]==0,1,jnp.where(bucket[0]==1,2,4)).astype(jnp.int32)
    zero=jnp.zeros((),jnp.int32)
    scal=jnp.stack([t.astype(jnp.int32),span,row_counts[0]]+[lengths[0,r] for r in range(lengths.shape[1])]+[zero]*(13-lengths.shape[1])+[(t*T).astype(jnp.int32)])
    g1=gain_one.reshape(1,D); g2=gain_two.reshape(1,D)
    lift=np.ones((1,3,1),np.float32); lift[0,0]=HD**-0.5
    w_pad=jnp.pad(w_qkv*jnp.asarray(lift,BF),((0,0),(0,0),(0,wide-C))).reshape(D,3*wide)

    normed=first_norm(stream,g1)
    far=swap(normed,"tensor",2); near=swap(normed,"tensor",1)
    own_w=jnp.concatenate([w_out,w_up,w_down],axis=0)
    near_w=swap(own_w,"tensor",1)
    packed=project(scal,normed,w_pad,n,0)
    near,near_w=lax.optimization_barrier((near,near_w))
    packed=project(scal,near,w_pad,n,1,packed)
    far,packed=lax.optimization_barrier((far,packed))
    far_w=swap(after(own_w,far),"tensor",2)
    corner=swap(far,"tensor",1)
    packed=project(scal,far,w_pad,n,2,packed)
    packed=project(scal,corner,w_pad,n,3,packed)
    *heads_out,qx=attn_fwd(scal,packed,T,nh)
    attn=[heads_out[0]]+[swap(heads_out[d],"tensor",d) for d in range(1,n)]
    weights=[own_w,near_w,far_w,swap(after(far_w,attn[1]),"tensor",1)]
    *grad_heads,result,mid,w_send,w_keep,go,sums=middle_part(scal,stream,cotangent,g2,attn,weights)
    heads=[grad_heads[0]]+[swap(grad_heads[d],"tensor",d) for d in range(1,n)]
    w_send,go_send=lax.optimization_barrier((w_send,go[:n//2],heads[1]))[:2]
    w_got=swap(w_send,"tensor",1); o_got=swap(go_send,"tensor",1)
    R=C+w_keep.shape[1]; q=lax.axis_size("dp"); r=R//q
    flat=lambda x: x.reshape(q,-1,D)
    w_half=(w_keep.astype(F32)+w_got.astype(F32)).astype(BF); o_half=(go[n//2:].astype(F32)+o_got.astype(F32)).astype(BF)
    w_half=jnp.concatenate([flat(x) for i in range(2) for x in (o_half[i],w_half[i,:D],w_half[i,D:])],axis=1).reshape(2*R,D)
    w_part=lax.psum_scatter(w_half,"dp",scatter_dimension=0,tiled=True)

    grad_packed=attn_bwd(scal,qx,packed,heads_out,heads,T,nh,list(range(nh)))
    gathered=jnp.concatenate([normed,near,far,corner],axis=0)
    w_part,grad_packed=lax.optimization_barrier((w_part,grad_packed))
    w_other=swap(w_part[r:],"tensor",2)
    gq=dot(gathered,grad_packed,TN)
    gq=(gq.reshape(D,3,wide)[:,:,:C]*lift).reshape(D,3*C)
    w_own=(w_part[:r].astype(F32)+w_other.astype(F32)).astype(BF)
    gq,w_own,grad_packed=lax.optimization_barrier((gq,w_own,grad_packed))
    w_sum=lax.all_gather(w_own,"dp",axis=0).astype(F32)
    gain_part=jnp.sum(gq.reshape(D,3,C)*w_qkv.astype(F32),axis=(1,2))/gain_one
    def back(i): return dot(grad_packed[i*T:(i+1)*T],w_pad,NT).astype(BF)
    groups=bit_groups(q)
    stage=scatter_stage(gq,"dp",groups[0])
    back_1,back_3=back(1),back(3)
    stage,back_1,back_3,grad_packed=lax.optimization_barrier((stage,back_1,back_3,grad_packed))
    near_0=swap(back_1,"tensor",1); near_2=swap(back_3,"tensor",1)
    back_2=back(2)
    two=(back_2.astype(F32)+near_2.astype(F32)).astype(BF)
    stage,two,grad_packed=lax.optimization_barrier((stage,two,grad_packed))
    far_b=swap(two,"tensor",2)
    for bits in groups[1:]: stage=scatter_stage(stage,"dp",bits)
    stage=stage.astype(BF); scattered=stage
    for bits in groups[:0:-1]: stage=gather_stage(stage,"dp",bits)
    back_0=back(0)
    grad_stream=last_norm(stream,mid,[back_0,near_0,far_b],g1)
    stage,grad_stream=lax.optimization_barrier((stage,grad_stream))
    gq=gather_stage(stage,"dp",groups[0]).astype(F32).reshape(D,3,C)
    cut=[0]
    for part in (C,D,w_keep.shape[1]-D): cut.append(cut[-1]+part//q)
    g_out,g_up,g_down=[w_sum[:,i:j].reshape(-1,D) for i,j in zip(cut[:-1],cut[1:])]
    group_tokens=jnp.sum(jnp.where(jnp.arange(lengths.shape[1])<row_counts[0],lengths[0],0)).astype(F32)/n
    s=sums.reshape(4,8,D)
    small=jnp.concatenate([gain_part,jnp.sum(s[0],axis=0),jnp.sum(s[1:],axis=(1,2)),group_tokens[None]])
    small=jnp.pad(small,(0,-small.shape[0]%LANES)).reshape(-1,LANES)
    small=after(small,scattered)
    small=butterfly(butterfly(small,"tensor"),"dp").reshape(-1)
    root=jnp.sqrt(small[2*D:2*D+3]/(D*small[2*D+3]))
    return (result,grad_stream,gq,g_out,g_up,g_down,small[:D],small[D:2*D],root)


def solution(mesh):
    rows=P(("dp","tensor"),None)
    return jax.shard_map(shards,mesh=mesh,
        in_specs=(rows,rows,P("dp"),P("dp"),P("dp",None),P(None,None,"tensor"),P("tensor",None),P(None,"tensor"),P("tensor",None),P(),P()),
        out_specs=(rows,rows,P(None,None,"tensor"),P("tensor",None),P(None,"tensor"),P("tensor",None),P(),P(),P()),
        check_vma=False)
```
